128 devices in a mesh: row: 16 (over z, y_hi, core), col: 8 (over y_lo, x).
Axes of the slice: x: 4, y: 4 (y_hi: 2, y_lo: 2; y = y_hi * 2 + y_lo), z: 4, core: 2. Of those that a mesh axis runs over, the one named last changes fastest.
Arguments:
- panel_left: bfloat16 [16, 4, 1024, 256], P('row', None, 'col'), may hold values from -0.375 to 0.375
- panel_right: bfloat16 [16, 4, 1024, 256], P('row', None, 'col'), may hold values from -1 to 1
- panel_ranks: int32 [16, 4], P('row'), may hold values from 64 to 256
- dense_mask: int32 [16, 8, 4, 8], P('row', 'col'), may hold values from 0 to 1, as said below
- dense_tiles: bfloat16 [16, 8, 4, 1024, 1024], P('row', 'col'), may hold values from -12 to 12
Outputs:
- update_core: bfloat16 [16, 8, 4, 8, 256, 256], P('row', 'col')
- dense_out: bfloat16 [16, 8, 4, 1024, 1024], P('row', 'col')
The draws below stay inside these ranges and needn't reach their ends.
Inputs may be any that keep to these rules, and one draw needn't show every extreme that they name: `dense_mask`: dense tiles lie only where i - j is 0, 1 or 2, always where it is 0 or 1; a device holds at most one dense tile in each of its tile rows.
All inputs are finite; a program needn't handle non-finite values.
Results may differ from the reference program's by a relative error of at most 0.0042.
Values may be sent and summed in bfloat16 or wider, within the bound.
A program may use at most 128 MiB of HBM per device.

```python
import jax
import jax.numpy as jnp
from jax import lax

NB = 1024
RMAX = 256
NT = 64
LR = 4
LC = 8
N_ROW = 16
N_COL = 8


def draw_dense_mask(key, part):
    key = jax.random.fold_in(key, 7)
    coins = jax.random.randint(key, (N_ROW, N_COL, LR, LC), 0, 2)
    tile_rows = jnp.arange(N_ROW)[:, None, None, None] + N_ROW * jnp.arange(LR)[None, None, :, None]
    tile_cols = jnp.arange(N_COL)[None, :, None, None] + N_COL * jnp.arange(LC)[None, None, None, :]
    offset = tile_rows - tile_cols
    banded = (offset >= 0) & (offset <= 1)
    extra = (offset == 2) & (coins == 1)
    return jnp.where(banded | extra, 1, 0).astype(jnp.int32)


def with_ends(array, key, smallest, high):
    spot = [jax.random.randint(jax.random.fold_in(key, axis), (), 0, length) for axis, length in enumerate(array.shape)]
    widest = array.shape.index(max(array.shape))
    beside = spot[:widest] + [(spot[widest] + 1) % array.shape[widest]] + spot[widest + 1:]
    return array.at[tuple(spot)].set(smallest).at[tuple(beside)].set(high)


def block_scale(stream_key, extent, pieces, low, top_value):
    def one(axis_at, parts):
        steps = jax.random.uniform(jax.random.fold_in(jax.random.fold_in(stream_key, 6), axis_at), (parts,), jnp.float32, low / len(pieces), top_value / len(pieces))
        return jnp.repeat(jnp.exp(steps), extent[axis_at] // parts).reshape((-1,) + (1,) * (len(extent) - axis_at - 1))

    gain = one(*pieces[0])
    for cut in pieces[1:]:
        gain = gain * one(*cut)
    return gain


def gaussian(own_key, shape, width, most, pieces=(), kind=jnp.bfloat16):
    entries = jax.random.normal(own_key, shape, jnp.float32) * width
    if len(pieces) > 0:
        entries = block_scale(own_key, shape, pieces, -0.22, 0.18) * entries
    return jnp.clip(entries, min=-most, max=most).astype(kind)


def setup_inputs(seed: int = 0) -> dict:
    arg_keys = jax.random.split(jax.random.key(seed), 6)
    panel_left = gaussian(arg_keys[0], (N_ROW, LR, NB, RMAX), RMAX ** -0.5, 0.375, ((0, 16), (2, 8)))
    panel_right = gaussian(arg_keys[1], (N_ROW, LR, NB, RMAX), (NB // 32) ** -0.5, 1.0, ((0, 16), (2, 8)))
    panel_ranks = with_ends(jax.random.randint(arg_keys[2], (N_ROW, LR), RMAX // 4, RMAX + 1), jax.random.fold_in(arg_keys[2], 1), RMAX // 4, RMAX).astype(jnp.int32)
    dense_mask = draw_dense_mask(jax.random.fold_in(arg_keys[5], 71), 0)
    dense_tiles = gaussian(arg_keys[4], (N_ROW, N_COL, LR, NB, NB), 2.0, 12.0, ((0, 16), (1, 8)))
    return dict(panel_left=panel_left, panel_right=panel_right, panel_ranks=panel_ranks, dense_mask=dense_mask, dense_tiles=dense_tiles)


def reference(panel_left, panel_right, panel_ranks, dense_mask, dense_tiles):
    kept_rank = jnp.arange(RMAX, dtype=jnp.int32)[None, None, :] < panel_ranks[:, :, None]
    zero_half = jnp.zeros((), jnp.bfloat16)
    left_all = jnp.where(kept_rank[:, :, None, :], panel_left, zero_half)
    right_all = jnp.where(kept_rank[:, :, None, :], panel_right, zero_half)
    left_tiles = left_all.transpose(1, 0, 2, 3).reshape(NT, NB, RMAX)
    right_wide = right_all.transpose(1, 0, 2, 3).reshape(NT, NB, RMAX).astype(jnp.float32)
    col_offsets = jnp.arange(LC, dtype=jnp.int32)
    col_starts = jnp.arange(N_COL, dtype=jnp.int32)

    def per_row(row_at):
        tile_rows = jnp.arange(LR, dtype=jnp.int32) * N_ROW + row_at
        row_right = right_wide[tile_rows]
        middle = jnp.einsum("ina,jnb->ijab", row_right, right_wide).astype(jnp.bfloat16)
        blocks = middle.reshape(LR, LC, N_COL, RMAX, RMAX).transpose(2, 0, 1, 3, 4)
        tile_cols = col_offsets[None, :] * N_COL + col_starts[:, None]
        dense_here = dense_mask[row_at]
        lower_rank = (tile_rows[None, :, None] >= tile_cols[:, None, :]) & (dense_here == 0)
        core_block = jnp.where(lower_rank[..., None, None], blocks, zero_half)
        has_dense = jnp.sum(dense_here, axis=2)
        chosen = jnp.sum(dense_here * col_offsets[None, None, :], axis=2).astype(jnp.int32)
        middle_pick = jnp.take_along_axis(blocks, chosen[:, :, None, None, None], axis=2)[:, :, 0]
        picked_cols = chosen * N_COL + col_starts[:, None]
        col_pick = left_tiles[picked_cols].astype(jnp.float32)
        row_left = left_tiles[tile_rows].astype(jnp.float32)
        narrow = jnp.einsum("lna,clab->clnb", row_left, middle_pick.astype(jnp.float32)).astype(jnp.bfloat16)
        change = jnp.einsum("clnb,clmb->clnm", narrow.astype(jnp.float32), col_pick)
        updated = (dense_tiles[row_at].astype(jnp.float32) - change).astype(jnp.bfloat16)
        dense_block = jnp.where((has_dense > 0)[:, :, None, None], updated, zero_half)
        return core_block, dense_block

    core_out, dense_out = lax.map(per_row, jnp.arange(N_ROW, dtype=jnp.int32))
    return core_out, dense_out
```

```python
import functools
import jax, jax.numpy as jnp
from jax import lax
from jax.experimental import pallas as pl
from jax.experimental.pallas import tpu as pltpu
from jax.sharding import PartitionSpec as P
MESH = pl.DeviceIdType.MESH

def gather_kernel(left_ref, right_ref, rank_ref, R, C, L, J,
                  row_s, row_r, col_s, col_r, mir_s, mir_r, half_s, half_r, core_s, core_r,
                  left_s, left_r, next_s, next_r, twin_s, twin_r, own_s, *, opts):
    r, c = lax.axis_index("row"), lax.axis_index("col")
    z, yh, core = r // 4, (r // 2) % 2, r % 2
    yl, x = c // 4, c % 4
    ahead, behind = yl * 4 + (x + 1) % 4, yl * 4 + (x + 3) % 4
    across = (1 - yl) * 4 + x
    up = ((z + 1) % 4) * 4 + yh * 2 + core
    down = ((z + 3) % 4) * 4 + yh * 2 + core
    mirror = z * 4 + (1 - yh) * 2 + core
    twin = z * 4 + yh * 2 + 1 - core
    gap = (r + 8 - c) % 8
    nxt, prv = (r + 2) % 16, (r + 14) % 16

    lane = lax.broadcasted_iota(jnp.int32, (128, 256), 1)
    for li in range(4):
        kept = lane < rank_ref[0, li]
        zero = jnp.zeros((128, 256), jnp.bfloat16)
        R[c, li] = jnp.where(kept, right_ref[0, li], zero)
        L[c, li] = jnp.where(kept, left_ref[0, li], zero)

    barrier = pltpu.get_barrier_semaphore()
    partners = [(r, (c + k) % 8) for k in range(1, 8)] + [(up, c), (down, c), (mirror, c), (twin, c), (nxt, c), (prv, c)]
    for p in partners:
        pl.semaphore_signal(barrier, inc=1, device_id=p, device_id_type=MESH)
    pl.semaphore_wait(barrier, len(partners))

    def send(src, dst, ss, rs, to):
        return pltpu.make_async_remote_copy(src_ref=src, dst_ref=dst, send_sem=ss, recv_sem=rs, device_id=to, device_id_type=MESH)

    order = [c, across, behind, ahead, (1 - yl) * 4 + (x + 3) % 4, (1 - yl) * 4 + (x + 1) % 4, yl * 4 + (x + 2) % 4, (1 - yl) * 4 + (x + 2) % 4]
    lo, hi = pl.ds(0, 2), pl.ds(2, 2)

    def row_copy(k, blk, part, to):
        v = R.at[blk] if part is None else R.at[blk, part]
        return send(v, v, row_s.at[k], row_r.at[k], (r, to))

    row = [
        row_copy(0, order[0], None, across), row_copy(1, order[0], None, ahead), row_copy(2, order[0], None, behind),
        row_copy(3, order[1], None, ahead), row_copy(4, order[1], None, behind),
        row_copy(5, order[2], lo, ahead), row_copy(6, order[3], hi, behind),
        row_copy(7, order[4], lo, ahead), row_copy(8, order[5], hi, behind)]
    got = [
        row_copy(0, order[1], None, across), row_copy(1, order[2], None, ahead), row_copy(2, order[3], None, behind),
        row_copy(3, order[4], None, ahead), row_copy(4, order[5], None, behind),
        row_copy(5, order[6], lo, ahead), row_copy(6, order[6], hi, behind),
        row_copy(7, order[7], lo, ahead), row_copy(8, order[7], hi, behind)]

    active = core == x % 2
    even = z % 2 == yl
    home = yh == x // 2
    source = active & even & home
    reflect = active & even & jnp.logical_not(home)
    odd = active & (z % 2 != yl)
    mine, other = z // 2, 1 - z // 2
    below, above = ((z + 3) % 4) // 2, ((z + 1) % 4) // 2

    def to_up(k, s): return send(R.at[order[k]], C.at[s, order[k]], col_s.at[0, k], col_r.at[0, k], (up, c))
    def to_down(k, s): return send(R.at[order[k]], C.at[s, order[k]], col_s.at[1, k], col_r.at[1, k], (down, c))
    def to_mirror(k, s): return send(R.at[order[k]], C.at[s, order[k]], mir_s.at[k], mir_r.at[k], (mirror, c))
    def from_mirror_up(k, s): return send(C.at[s, order[k]], C.at[s, order[k]], col_s.at[0, k], col_r.at[0, k], (up, c))
    def from_mirror_down(k, s): return send(C.at[s, order[k]], C.at[s, order[k]], col_s.at[1, k], col_r.at[1, k], (down, c))
    def half_up(k, s): return send(C.at[s, order[k], lo], C.at[s, order[k], lo], half_s.at[0, k], half_r.at[0, k], (up, c))
    def half_down(k, s): return send(C.at[s, order[k], hi], C.at[s, order[k], hi], half_s.at[1, k], half_r.at[1, k], (down, c))
    def to_twin(k, s, t): return send(C.at[s, order[k]], C.at[s, order[k]], core_s.at[t, k], core_r.at[t, k], (twin, c))
    def own(k): return pltpu.make_async_copy(R.at[order[k]], C.at[mine, order[k]], own_s.at[k])

    def col_source(k):
        @pl.when(source)
        def _():
            to_up(k, mine).start(); to_down(k, mine).start(); to_mirror(k, mine).start()
            own(k).start()
            send(R.at[order[k]], C.at[mine, order[k]], core_s.at[0, k], core_r.at[0, k], (twin, c)).start()

    def col_mirror(k):
        @pl.when(reflect)
        def _():
            to_mirror(k, mine).wait_recv()
            from_mirror_up(k, mine).start(); from_mirror_down(k, mine).start()
            to_twin(k, mine, 0).start()

    def col_odd(k):
        @pl.when(odd)
        def _():
            from_mirror_up(k, below).wait_recv()
            half_up(k, below).start()
            to_twin(k, below, 0).start()
            from_mirror_down(k, above).wait_recv()
            half_down(k, above).start()
            to_twin(k, above, 1).start()

    def col_last(k):
        @pl.when(active & even)
        def _():
            half_up(k, other).wait_recv(); half_down(k, other).wait_recv()
            to_twin(k, other, 1).start()

    def col_end(k):
        @pl.when(source)
        def _():
            to_up(k, mine).wait_send(); to_down(k, mine).wait_send(); to_mirror(k, mine).wait_send()
            own(k).wait()
        @pl.when(reflect)
        def _():
            from_mirror_up(k, mine).wait_send(); from_mirror_down(k, mine).wait_send()
        @pl.when(odd)
        def _():
            half_up(k, below).wait_send(); half_down(k, above).wait_send()
        @pl.when(active)
        def _():
            to_twin(k, mine, 0).wait_send(); to_twin(k, other, 1).wait_send()
        @pl.when(jnp.logical_not(active))
        def _():
            @pl.when(even)
            def _():
                to_twin(k, mine, 0).wait_recv(); to_twin(k, other, 1).wait_recv()
            @pl.when(jnp.logical_not(even))
            def _():
                to_twin(k, below, 0).wait_recv(); to_twin(k, above, 1).wait_recv()

    def left_copy(t, blk, to): return send(L.at[blk], L.at[blk], left_s.at[t], left_r.at[blk], (r, to))
    def left_start():
        for t in range(3):
            to = (r + 8 - t) % 8
            @pl.when(to != c)
            def _():
                left_copy(t, c, to).start()
    def left_end():
        for t in range(3):
            to = (r + 8 - t) % 8
            @pl.when(to != c)
            def _():
                left_copy(t, c, to).wait_send()
    def onward(k): return send(L.at[order[k]], J.at[order[k]], next_s.at[k], next_r.at[k], (nxt, c))
    def l_twin(k): return send(L.at[order[k]], J.at[order[k]], twin_s.at[k], twin_r.at[k], (twin, c))
    def j_twin(k): return send(J.at[order[k]], J.at[order[k]], twin_s.at[k], twin_r.at[k], (twin, c))
    def left_step(k):
        if k > 0:
            @pl.when(gap <= 2)
            def _():
                left_copy(0, order[k], c).wait_recv()
        @pl.when(gap == 0)
        def _():
            onward(k).start()
        @pl.when((gap == 0) & (core == 0))
        def _():
            l_twin(k).start()
    def next_step(k):
        @pl.when(gap == 2)
        def _():
            onward(k).wait_recv()
        @pl.when((gap == 2) & (core == 1))
        def _():
            j_twin(k).start()
    def next_end(k):
        @pl.when(gap == 0)
        def _():
            onward(k).wait_send()
        @pl.when(((gap == 0) & (core == 0)) | ((gap == 2) & (core == 1)))
        def _():
            l_twin(k).wait_send()
        @pl.when(gap == 1)
        def _():
            j_twin(k).wait_recv()

    do_col, do_left = opts.get("col", True), opts.get("left", True)
    lag1, lag2, lagl, lagn = opts.get("lags", (1, 2, 2, 4))
    left_at = opts.get("left_at", 0)
    for cp in row[:3]:
        cp.start()
    K = 8
    for k in range(K + max(lag1, lag2, lagl, lagn) + 1):
        if k < K:
            if k == 1:
                got[0].wait_recv(); row[3].start(); row[4].start()
            elif k == 2:
                got[1].wait_recv(); row[5].start()
            elif k == 3:
                got[2].wait_recv(); row[6].start()
            elif k == 4:
                got[3].wait_recv(); row[7].start()
            elif k == 5:
                got[4].wait_recv(); row[8].start()
            elif k == 6:
                got[5].wait_recv(); got[6].wait_recv()
            elif k == 7:
                got[7].wait_recv(); got[8].wait_recv()
            if do_col:
                col_source(k)
        if do_left and k == left_at:
            left_start()
        if do_col:
            if 0 <= k - lag1 < K:
                col_mirror(k - lag1)
                col_odd(k - lag1)
            if 0 <= k - lag2 < K:
                col_last(k - lag2)
        if do_left:
            if 0 <= k - lagl < K:
                left_step(k - lagl)
            if 0 <= k - lagn < K:
                next_step(k - lagn)
    for cp in row:
        cp.wait_send()
    if do_left:
        left_end()
    for k in range(K):
        if do_col:
            col_end(k)
        if do_left:
            next_end(k)


def gather(panel_left, panel_right, panel_ranks, opts={}, vm=pltpu.VMEM):
    bf = jnp.bfloat16
    V = pl.BlockSpec(memory_space=vm)
    D = lambda *s: pltpu.SemaphoreType.DMA(s)
    return pl.pallas_call(
        functools.partial(gather_kernel, opts=opts),
        out_shape=(jax.ShapeDtypeStruct((8, 4, 128, 256), bf), jax.ShapeDtypeStruct((2, 8, 4, 128, 256), bf),
                   jax.ShapeDtypeStruct((8, 4, 128, 256), bf), jax.ShapeDtypeStruct((8, 4, 128, 256), bf)),
        in_specs=[pl.BlockSpec(memory_space=pltpu.VMEM)] * 2 + [pl.BlockSpec(memory_space=pltpu.SMEM)],
        out_specs=(V, V, V, V),
        scratch_shapes=[D(9), D(9), D(2, 8), D(2, 8), D(8), D(8), D(2, 8), D(2, 8), D(2, 8), D(2, 8), D(3), D(8), D(8), D(8), D(8), D(8), D(8)],
        compiler_params=pltpu.CompilerParams(collective_id=0, has_side_effects=True, vmem_limit_bytes=60 << 20),
        name="gather_panels",
    )(panel_left, panel_right, panel_ranks)


def update_kernel(R, C, L, J, mask_ref, tiles, core_out, dense_out,
                  flipped, cores, masked, dense, panels, lean, tile_sem, core_sem, dense_sem):
    r, c = lax.axis_index("row"), lax.axis_index("col")
    gap = (r + 8 - c) % 8
    has_tiles = gap <= 2
    shift = (r - gap - c) // 8

    def tile_in(li): return pltpu.make_async_copy(tiles.at[0, 0, li], dense.at[li], tile_sem.at[li])
    def core_back(lj): return pltpu.make_async_copy(masked.at[:, lj], core_out.at[0, 0, :, lj], core_sem.at[lj])
    def dense_back(li): return pltpu.make_async_copy(dense.at[li], dense_out.at[0, 0, li], dense_sem.at[li])
    def zero_back(li): return pltpu.make_async_copy(dense.at[0], dense_out.at[0, 0, li], dense_sem.at[li])

    @pl.when(has_tiles)
    def _():
        for li in range(4):
            tile_in(li).start()

    @pl.when(jnp.logical_not(has_tiles))
    def _():
        dense[0] = jnp.zeros((1024, 1024), jnp.bfloat16)
        for li in range(4):
            zero_back(li).start()

    for li in range(4):
        flipped[li] = R[:, li].reshape(1024, 256).T
    for lj in range(8):
        first = lj // 2
        right_j = C[lj % 2, :, first].reshape(1024, 256)
        wide = jnp.dot(flipped[first:].reshape((4 - first) * 256, 1024), right_j, preferred_element_type=jnp.float32)
        wide = wide.astype(jnp.bfloat16).reshape(4 - first, 256, 256)
        for li in range(4):
            if li < first:
                masked[li, lj] = jnp.zeros((256, 256), jnp.bfloat16)
            else:
                cores[li, lj] = wide[li - first]
                keep = (li * 16 + r >= lj * 8 + c) & (mask_ref[0, 0, li, lj] == 0)
                masked[li, lj] = jnp.where(keep, wide[li - first], jnp.zeros((256, 256), jnp.bfloat16))
        core_back(lj).start()

    @pl.when(has_tiles)
    def _():
        for li in range(4):
            lj = 2 * li + shift
            there = (lj >= 0) & (mask_ref[0, 0, li, jnp.maximum(lj, 0)] > 0)
            lj = jnp.maximum(lj, 0)
            back = jnp.where(r < gap, 1, 0)
            lj_row = jnp.maximum(li - back, 0)
            lean[...] = jnp.dot(L[:, li].reshape(1024, 256), cores[li, lj], preferred_element_type=jnp.float32).astype(jnp.bfloat16)

            @pl.when(gap == 0)
            def _():
                panels[...] = L[:, li].reshape(1024, 256)

            @pl.when(gap > 0)
            def _():
                panels[...] = J[:, lj_row].reshape(1024, 256)
            tile_in(li).wait()
            for part in range(4):
                rows = pl.ds(part * 256, 256)
                change = lax.dot_general(lean[rows], panels[...], (((1,), (1,)), ((), ())), preferred_element_type=jnp.float32)
                new = (dense[li, rows].astype(jnp.float32) - change).astype(jnp.bfloat16)
                dense[li, rows] = jnp.where(there, new, jnp.zeros_like(new))
            dense_back(li).start()

    for lj in range(8):
        core_back(lj).wait()
    for li in range(4):
        dense_back(li).wait()


def update(R, C, L, J, dense_mask, dense_tiles, vm=pltpu.VMEM):
    bf = jnp.bfloat16
    V = pl.BlockSpec(memory_space=vm)
    A = pl.BlockSpec(memory_space=pl.ANY)
    return pl.pallas_call(
        update_kernel,
        out_shape=(jax.ShapeDtypeStruct((1, 1, 4, 8, 256, 256), bf), jax.ShapeDtypeStruct((1, 1, 4, 1024, 1024), bf)),
        in_specs=[V, V, V, V, pl.BlockSpec(memory_space=pltpu.SMEM), A],
        out_specs=(A, A),
        scratch_shapes=[pltpu.VMEM((4, 256, 1024), bf), pltpu.VMEM((4, 8, 256, 256), bf), pltpu.VMEM((4, 8, 256, 256), bf),
                        pltpu.VMEM((4, 1024, 1024), bf), pltpu.VMEM((1024, 256), bf), pltpu.VMEM((1024, 256), bf),
                        pltpu.SemaphoreType.DMA((4,)), pltpu.SemaphoreType.DMA((8,)), pltpu.SemaphoreType.DMA((4,))],
        compiler_params=pltpu.CompilerParams(vmem_limit_bytes=60 << 20),
        name="update_tiles",
    )(R, C, L, J, dense_mask, dense_tiles)


def per_device(panel_left, panel_right, panel_ranks, dense_mask, dense_tiles):
    R, C, L, J = gather(panel_left, panel_right, panel_ranks)
    return update(R, C, L, J, dense_mask, dense_tiles)


def solution(mesh):
    placed = (
        P("row", None, "col", None),
        P("row", None, "col", None),
        P("row", None),
        P("row", "col", None, None),
        P("row", "col", None, None, None),
    )
    return jax.shard_map(
        per_device,
        mesh=mesh,
        in_specs=placed,
        out_specs=(P("row", "col", None, None, None, None), P("row", "col", None, None, None)),
        check_vma=False,
    )
```

```python
import functools
import jax, jax.numpy as jnp
from jax import lax
from jax.experimental import pallas as pl
from jax.experimental.pallas import tpu as pltpu
from jax.sharding import PartitionSpec as P
MESH = pl.DeviceIdType.MESH
ORDER = ["r0", "r1", "r2", "r3", "m0", "r4", "r5", "S0", "Z0", "J0", "m1", "m2", "m3", "o0", "r6", "r7", "J1", "m4", "o1", "m5", "o2", "m6", "o3", "x0", "x1", "x2", "x3", "m7", "o4", "o5", "o6", "o7", "e0", "e1", "e2", "e3", "e4", "e5", "e6", "e7", "l0", "l1", "l2", "l3", "l4", "l5", "l6", "l7", "n0", "n1", "n2", "n3", "n4", "n5", "n6", "n7"]


def gather_kernel(left_ref, right_ref, rank_ref, R, C, L, J, XJ, ZB,
                  row_s, row_r, col_s, col_r, mir_r, core_s, core_r,
                  left_s, left_r, next_s, next_r, relay_s, relay_r, lift_s, lift_r, twin_s, twin_r, own_s, *, opts):
    r, c = lax.axis_index("row"), lax.axis_index("col")
    z, yh, core = r // 4, (r // 2) % 2, r % 2
    yl, x = c // 4, c % 4
    ahead, behind = yl * 4 + (x + 1) % 4, yl * 4 + (x + 3) % 4
    across = (1 - yl) * 4 + x
    up = ((z + 1) % 4) * 4 + yh * 2 + core
    down = ((z + 3) % 4) * 4 + yh * 2 + core
    mirror = z * 4 + (1 - yh) * 2 + core
    twin = z * 4 + yh * 2 + 1 - core
    gap = (r + 8 - c) % 8
    no = jnp.logical_not

    lane = lax.broadcasted_iota(jnp.int32, (128, 256), 1)
    for li in range(4):
        kept = lane < rank_ref[0, li]
        zero = jnp.zeros((128, 256), jnp.bfloat16)
        R[c, li] = jnp.where(kept, right_ref[0, li], zero)
        L[c, li] = jnp.where(kept, left_ref[0, li], zero)

    hand = across == (r + 14) % 8
    barrier = pltpu.get_barrier_semaphore()
    partners = [(r, (c + k) % 8) for k in range(1, 8)] + [(up, c), (down, c), (mirror, c), (twin, c)]
    for p in partners:
        pl.semaphore_signal(barrier, inc=1, device_id=p, device_id_type=MESH)

    @pl.when((gap == 2) | hand)
    def _():
        for j in range(4):
            pl.semaphore_signal(barrier, inc=1, device_id=(mirror, (1 - yl) * 4 + j), device_id_type=MESH)
    pl.semaphore_wait(barrier, len(partners) + 1)

    def send(src, dst, ss, rs, to):
        return pltpu.make_async_remote_copy(src_ref=src, dst_ref=dst, send_sem=ss, recv_sem=rs, device_id=to, device_id_type=MESH)

    order = [c, across, behind, ahead, (1 - yl) * 4 + (x + 3) % 4, (1 - yl) * 4 + (x + 1) % 4, yl * 4 + (x + 2) % 4, (1 - yl) * 4 + (x + 2) % 4]
    lo, hi = pl.ds(0, 2), pl.ds(2, 2)

    def row_copy(k, blk, part, to):
        v = R.at[blk] if part is None else R.at[blk, part]
        return send(v, v, row_s, row_r.at[k], (r, to))

    row = [
        row_copy(0, order[0], None, across), row_copy(1, order[0], None, ahead), row_copy(2, order[0], None, behind),
        row_copy(3, order[1], None, ahead), row_copy(4, order[1], None, behind),
        row_copy(5, order[2], lo, ahead), row_copy(6, order[3], hi, behind),
        row_copy(7, order[4], lo, ahead), row_copy(8, order[5], hi, behind)]
    got = [
        row_copy(0, order[1], None, across), row_copy(1, order[2], None, ahead), row_copy(2, order[3], None, behind),
        row_copy(3, order[4], None, ahead), row_copy(4, order[5], None, behind),
        row_copy(5, order[6], lo, ahead), row_copy(6, order[6], hi, behind),
        row_copy(7, order[7], lo, ahead), row_copy(8, order[7], hi, behind)]

    active = core == x % 2
    even = z % 2 == yl
    home = yh == x // 2
    source = active & even & home
    reflect = active & even & no(home)
    odd = active & (z % 2 != yl)
    mine, other = z // 2, 1 - z // 2
    below, above = ((z + 3) % 4) // 2, ((z + 1) % 4) // 2

    def c_copy(k, s, way, part=None):
        v = C.at[s, order[k]] if part is None else C.at[s, order[k], part]
        return send(v, v, col_s.at[way], col_r.at[way, k], ((up, down)[way], c))
    def r_copy(k, way): return send(R.at[order[k]], C.at[mine, order[k]], col_s.at[way], col_r.at[way, k], ((up, down)[way], c))
    def to_mirror(k): return send(R.at[order[k]], C.at[mine, order[k]], col_s.at[2], mir_r.at[k], (mirror, c))
    def to_twin(k, s, t): return send(C.at[s, order[k]], C.at[s, order[k]], core_s.at[t], core_r.at[t], (twin, c))
    def own(k): return pltpu.make_async_copy(R.at[order[k]], C.at[mine, order[k]], own_s.at[k])

    def col_source(k):
        @pl.when(source)
        def _():
            r_copy(k, 0).start(); r_copy(k, 1).start(); to_mirror(k).start()
            own(k).start()
            send(R.at[order[k]], C.at[mine, order[k]], core_s.at[0], core_r.at[0], (twin, c)).start()

    def row_step(k):
        if k == 1:
            got[0].wait_recv(); row[3].start(); row[4].start()
        elif k == 2:
            got[1].wait_recv(); row[5].start()
        elif k == 3:
            got[2].wait_recv(); row[6].start()
        elif k == 4:
            got[3].wait_recv(); row[7].start()
        elif k == 5:
            got[4].wait_recv(); row[8].start()
        elif k == 6:
            got[5].wait_recv(); got[6].wait_recv()
        elif k == 7:
            got[7].wait_recv(); got[8].wait_recv()
        if do_col:
            col_source(k)

    def col_mirror(k):
        @pl.when(reflect)
        def _():
            to_mirror(k).wait_recv()
            c_copy(k, mine, 0).start(); c_copy(k, mine, 1).start()
            to_twin(k, mine, 0).start()

    def col_odd(k):
        @pl.when(odd)
        def _():
            c_copy(k, below, 0).wait_recv()
            c_copy(k, below, 0, lo).start()
            to_twin(k, below, 0).start()
            c_copy(k, above, 1).wait_recv()
            c_copy(k, above, 1, hi).start()
            to_twin(k, above, 1).start()

    def col_last(k):
        @pl.when(active & even)
        def _():
            c_copy(k, other, 0, lo).wait_recv(); c_copy(k, other, 1, hi).wait_recv()
            to_twin(k, other, 1).start()

    def whole(s, ss, rs): return send(C.at[s], C.at[s], ss, rs, (twin, c))
    def some(s, n, ss, rs): return send(C.at[s, pl.ds(0, n)], C.at[s, pl.ds(0, n)], ss, rs, (twin, c))

    def col_end():
        @pl.when(active & even)
        def _():
            whole(mine, col_s.at[0], core_r.at[0]).wait_send()
            whole(mine, col_s.at[1], core_r.at[0]).wait_send()
        @pl.when(source)
        def _():
            whole(mine, col_s.at[2], core_r.at[0]).wait_send()
            for k in range(8):
                own(k).wait()
        @pl.when(odd)
        def _():
            some(0, 4, col_s.at[0], core_r.at[0]).wait_send()
            some(0, 4, col_s.at[1], core_r.at[0]).wait_send()
        @pl.when(active)
        def _():
            whole(0, core_s.at[0], core_r.at[0]).wait_send()
            whole(1, core_s.at[1], core_r.at[1]).wait_send()
        @pl.when(no(active) & even)
        def _():
            whole(mine, core_s.at[0], core_r.at[0]).wait_recv()
            whole(other, core_s.at[1], core_r.at[1]).wait_recv()
        @pl.when(no(active) & no(even))
        def _():
            whole(below, core_s.at[0], core_r.at[0]).wait_recv()
            whole(above, core_s.at[1], core_r.at[1]).wait_recv()

    def left_copy(t, blk, to): return send(L.at[blk], L.at[blk], left_s.at[t], left_r.at[blk], (r, to))
    def left_start(_k):
        for t in range(3):
            to = (r + 8 - t) % 8
            @pl.when(to != c)
            def _():
                left_copy(t, c, to).start()
    def left_end():
        for t in range(3):
            to = (r + 8 - t) % 8
            @pl.when(to != c)
            def _():
                left_copy(t, c, to).wait_send()
    def l_twin(k): return send(L.at[order[k]], J.at[order[k]], twin_s, twin_r, (twin, c))
    def j_twin(k): return send(J.at[order[k]], J.at[order[k]], twin_s, twin_r, (twin, c))
    def left_step(k):
        if k > 0:
            @pl.when(gap <= 2)
            def _():
                left_copy(0, order[k], c).wait_recv()
        @pl.when((gap == 0) & (core == 0))
        def _():
            l_twin(k).start()

    goal = jnp.where(yh == 0, r, r + 12) % 8
    same = goal // 4 == yl
    lift = send(L.at[c], ZB, lift_s, lift_r, (up, c))
    def lift_start(_k):
        @pl.when(yh == 1)
        def _():
            lift.start()
    def part_from(src):
        return (send(src, XJ.at[x], next_s, relay_r.at[x], (mirror, (1 - goal // 4) * 4 + goal % 4)),
                send(src, J.at[c], next_s, next_r.at[c], (mirror, goal)))
    def part_start(k):
        @pl.when(yh == k)
        def _():
            if k == 1:
                lift.wait_recv()
            by, direct = part_from(ZB if k == 1 else L.at[c])
            @pl.when(same)
            def _():
                by.start()
            @pl.when(no(same))
            def _():
                direct.start()
    def relay(j): return send(XJ.at[j], J.at[(1 - yl) * 4 + j], relay_s, next_r.at[(1 - yl) * 4 + j], (r, across))
    def relay_step(j):
        @pl.when(hand)
        def _():
            send(XJ.at[j], XJ.at[j], relay_s, relay_r.at[j], (r, across)).wait_recv()
            relay(j).start()
    def next_step(k):
        @pl.when(gap == 2)
        def _():
            send(J.at[order[k]], J.at[order[k]], relay_s, next_r.at[order[k]], (r, across)).wait_recv()
        @pl.when((gap == 2) & (core == 1))
        def _():
            j_twin(k).start()
    def next_end():
        part_from(L.at[c])[1].wait_send()
        @pl.when(yh == 1)
        def _():
            lift.wait_send()
        @pl.when(hand)
        def _():
            send(XJ, XJ, relay_s, lift_r, (r, across)).wait_send()
        @pl.when(((gap == 0) & (core == 0)) | ((gap == 2) & (core == 1)))
        def _():
            send(J, J, twin_s, twin_r, (twin, c)).wait_send()
        @pl.when(gap == 1)
        def _():
            send(J, J, twin_s, twin_r, (twin, c)).wait_recv()

    do_col, do_left = opts.get("col", True), opts.get("left", True)
    for cp in row[:3]:
        cp.start()
    steps = dict(r=row_step)
    if do_col:
        steps.update(m=col_mirror, o=col_odd, e=col_last)
    if do_left:
        steps.update(S=left_start, l=left_step, n=next_step, Z=lift_start, J=part_start, x=relay_step)
    words = opts.get("order", ORDER)
    for word in (words.split() if isinstance(words, str) else words):
        if word[0] in steps:
            steps[word[0]](int(word[1:]))
    send(R.at[pl.ds(0, 7)], R.at[pl.ds(0, 7)], row_s, lift_r, (twin, c)).wait_send()
    if do_left:
        left_end()
        next_end()
    if do_col:
        col_end()


bf = jnp.bfloat16
def D(*s): return pltpu.SemaphoreType.DMA(s)
SCRATCH = [pltpu.VMEM((4, 4, 128, 256), bf), pltpu.VMEM((4, 128, 256), bf),
           D(), D(9), D(3), D(2, 8), D(8), D(2), D(2),
           D(3), D(8), D(), D(8), D(), D(4), D(), D(), D(), D(), D(8)]
PANELS = [(8, 4, 128, 256), (2, 8, 4, 128, 256), (8, 4, 128, 256), (8, 4, 128, 256)]


def gather(panel_left, panel_right, panel_ranks, opts={}):
    V = pl.BlockSpec(memory_space=pltpu.VMEM)
    return pl.pallas_call(
        functools.partial(gather_kernel, opts=opts),
        out_shape=tuple(jax.ShapeDtypeStruct(s, bf) for s in PANELS),
        in_specs=[V, V, pl.BlockSpec(memory_space=pltpu.SMEM)],
        out_specs=(V, V, V, V),
        scratch_shapes=SCRATCH,
        compiler_params=pltpu.CompilerParams(collective_id=0, has_side_effects=True, vmem_limit_bytes=60 << 20),
        name="gather_panels",
    )(panel_left, panel_right, panel_ranks)


def update_kernel(R, C, L, J, mask_ref, tiles, core_out, dense_out,
                  flipped, cores, masked, dense, panels, lean, tile_sem, core_sem, dense_sem):
    r, c = lax.axis_index("row"), lax.axis_index("col")
    gap = (r + 8 - c) % 8
    has_tiles = gap <= 2
    shift = (r - gap - c) // 8

    def tile_in(li): return pltpu.make_async_copy(tiles.at[0, 0, li], dense.at[li], tile_sem.at[li])
    def core_back(lj): return pltpu.make_async_copy(masked.at[:, lj], core_out.at[0, 0, :, lj], core_sem.at[lj])
    def dense_back(li): return pltpu.make_async_copy(dense.at[li], dense_out.at[0, 0, li], dense_sem.at[li])
    def zero_back(li): return pltpu.make_async_copy(dense.at[0], dense_out.at[0, 0, li], dense_sem.at[li])

    @pl.when(has_tiles)
    def _():
        for li in range(4):
            tile_in(li).start()

    @pl.when(jnp.logical_not(has_tiles))
    def _():
        dense[0] = jnp.zeros((1024, 1024), jnp.bfloat16)
        for li in range(4):
            zero_back(li).start()

    for li in range(4):
        flipped[li] = R[:, li].reshape(1024, 256).T
    for lj in range(8):
        first = lj // 2
        right_j = C[lj % 2, :, first].reshape(1024, 256)
        wide = jnp.dot(flipped[first:].reshape((4 - first) * 256, 1024), right_j, preferred_element_type=jnp.float32)
        wide = wide.astype(jnp.bfloat16).reshape(4 - first, 256, 256)
        for li in range(4):
            if li < first:
                masked[li, lj] = jnp.zeros((256, 256), jnp.bfloat16)
            else:
                cores[li, lj] = wide[li - first]
                keep = (li * 16 + r >= lj * 8 + c) & (mask_ref[0, 0, li, lj] == 0)
                masked[li, lj] = jnp.where(keep, wide[li - first], jnp.zeros((256, 256), jnp.bfloat16))
        core_back(lj).start()

    @pl.when(has_tiles)
    def _():
        for li in range(4):
            lj = 2 * li + shift
            there = (lj >= 0) & (mask_ref[0, 0, li, jnp.maximum(lj, 0)] > 0)
            lj = jnp.maximum(lj, 0)
            back = jnp.where(r < gap, 1, 0)
            lj_row = jnp.maximum(li - back, 0)
            lean[...] = jnp.dot(L[:, li].reshape(1024, 256), cores[li, lj], preferred_element_type=jnp.float32).astype(jnp.bfloat16)

            @pl.when(gap == 0)
            def _():
                panels[...] = L[:, li].reshape(1024, 256)

            @pl.when(gap > 0)
            def _():
                panels[...] = J[:, lj_row].reshape(1024, 256)
            tile_in(li).wait()
            for part in range(4):
                rows = pl.ds(part * 256, 256)
                change = lax.dot_general(lean[rows], panels[...], (((1,), (1,)), ((), ())), preferred_element_type=jnp.float32)
                new = (dense[li, rows].astype(jnp.float32) - change).astype(jnp.bfloat16)
                dense[li, rows] = jnp.where(there, new, jnp.zeros_like(new))
            dense_back(li).start()

    for lj in range(8):
        core_back(lj).wait()
    for li in range(4):
        dense_back(li).wait()


def update(R, C, L, J, dense_mask, dense_tiles, vm=pltpu.VMEM):
    bf = jnp.bfloat16
    V = pl.BlockSpec(memory_space=vm)
    A = pl.BlockSpec(memory_space=pl.ANY)
    return pl.pallas_call(
        update_kernel,
        out_shape=(jax.ShapeDtypeStruct((1, 1, 4, 8, 256, 256), bf), jax.ShapeDtypeStruct((1, 1, 4, 1024, 1024), bf)),
        in_specs=[V, V, V, V, pl.BlockSpec(memory_space=pltpu.SMEM), A],
        out_specs=(A, A),
        scratch_shapes=[pltpu.VMEM((4, 256, 1024), bf), pltpu.VMEM((4, 8, 256, 256), bf), pltpu.VMEM((4, 8, 256, 256), bf),
                        pltpu.VMEM((4, 1024, 1024), bf), pltpu.VMEM((1024, 256), bf), pltpu.VMEM((1024, 256), bf),
                        pltpu.SemaphoreType.DMA((4,)), pltpu.SemaphoreType.DMA((8,)), pltpu.SemaphoreType.DMA((4,))],
        compiler_params=pltpu.CompilerParams(vmem_limit_bytes=60 << 20),
        name="update_tiles",
    )(R, C, L, J, dense_mask, dense_tiles)


def per_device(panel_left, panel_right, panel_ranks, dense_mask, dense_tiles):
    R, C, L, J = gather(panel_left, panel_right, panel_ranks)
    return update(R, C, L, J, dense_mask, dense_tiles)


def solution(mesh):
    placed = (
        P("row", None, "col", None),
        P("row", None, "col", None),
        P("row", None),
        P("row", "col", None, None),
        P("row", "col", None, None, None),
    )
    return jax.shard_map(
        per_device,
        mesh=mesh,
        in_specs=placed,
        out_specs=(P("row", "col", None, None, None, None), P("row", "col", None, None, None)),
        check_vma=False,
    )
```

```python
import functools
import jax, jax.numpy as jnp
from jax import lax
from jax.experimental import pallas as pl
from jax.experimental.pallas import tpu as pltpu
from jax.sharding import PartitionSpec as P
MESH = pl.DeviceIdType.MESH
NY = 2
ORDER = ["r0", "s0", "M0", "r2", "r3", "s2", "s3", "r1", "s1", "o0", "s6", "o2", "o3", "S0", "c0", "Z0", "c2", "r5", "r4", "s4", "J0", "o6", "J1", "s5", "S2", "S1", "c1", "o4", "s7", "d2", "d0", "o1", "d1", "x0", "x2", "c3", "x3", "o5", "T0", "x1", "h1", "h0", "d3", "e3", "l0", "o7", "h2", "h3", "e2", "e1", "e0", "e6", "e5", "l2", "e4", "e7", "q0", "l1", "l3", "n3", "l4", "l6", "n1", "n5", "n2", "n4", "n7", "n6", "l5", "n0", "l7"]


def gather_kernel(left_in, right_in, rank_in, R, C, L, J, XJ, ZB, OWN, raw, rank_ref, load_s,
                  row_s, row_r, col_s, col_r, mir_r, core_s, core_r,
                  left_s, left_r, next_s, next_r, relay_s, relay_r, lift_s, lift_r, twin_s, twin_r, own_s, keep_s, over_s, over_r, on_s, on_r, hold_s, *, opts):
    r, c = lax.axis_index("row"), lax.axis_index("col")
    z, yh, core = r // 4, (r // 2) % 2, r % 2
    yl, x = c // 4, c % 4
    ahead, behind = yl * 4 + (x + 1) % 4, yl * 4 + (x + 3) % 4
    across = (1 - yl) * 4 + x
    up = ((z + 1) % 4) * 4 + yh * 2 + core
    down = ((z + 3) % 4) * 4 + yh * 2 + core
    mirror = z * 4 + (1 - yh) * 2 + core
    twin = z * 4 + yh * 2 + 1 - core
    gap = (r + 8 - c) % 8
    no = jnp.logical_not

    loads = [pltpu.make_async_copy(rank_in, rank_ref, load_s.at[2]),
             pltpu.make_async_copy(right_in.at[0], raw.at[0], load_s.at[0]), pltpu.make_async_copy(left_in.at[0], raw.at[1], load_s.at[1])]
    for cp in loads:
        cp.start()

    hand = across == (r + 14) % 8
    active = core == x % 2
    even = z % 2 == yl
    home = yh == x // 2
    source = active & even & home
    odd = active & no(even) & home
    far = active & no(home)
    aside = (r % 8) // 4 != yl
    barrier = pltpu.get_barrier_semaphore()
    partners = [(r, (c + k) % 8) for k in range(1, 8)] + [(up, c), (down, c), (mirror, c), (twin, c)]
    for p in partners:
        pl.semaphore_signal(barrier, inc=1, device_id=p, device_id_type=MESH)

    @pl.when(far & even)
    def _():
        for j in range(4):
            pl.semaphore_signal(barrier, inc=1, device_id=(mirror, (1 - yl) * 4 + j), device_id_type=MESH)

    @pl.when((gap == 2) | hand)
    def _():
        for j in range(4):
            pl.semaphore_signal(barrier, inc=1, device_id=(mirror, (1 - yl) * 4 + j), device_id_type=MESH)
    for cp in loads:
        cp.wait()
    lane = lax.broadcasted_iota(jnp.int32, (128, 256), 1)
    for li in range(4):
        kept = lane < rank_ref[0, li]
        zero = jnp.zeros((128, 256), jnp.bfloat16)
        OWN[0, li] = jnp.where(kept, raw[0, li], zero)
        OWN[1, li] = jnp.where(kept, raw[1, li], zero)
    keep = [pltpu.make_async_copy(OWN.at[0], R.at[c], keep_s.at[0]), pltpu.make_async_copy(OWN.at[1], L.at[c], keep_s.at[1])]
    for cp in keep:
        cp.start()

    pl.semaphore_wait(barrier, len(partners) + 1 + jnp.where(aside, 1, 0))

    def send(src, dst, ss, rs, to):
        return pltpu.make_async_remote_copy(src_ref=src, dst_ref=dst, send_sem=ss, recv_sem=rs, device_id=to, device_id_type=MESH)

    order = [c, across, behind, ahead, (1 - yl) * 4 + (x + 3) % 4, (1 - yl) * 4 + (x + 1) % 4, yl * 4 + (x + 2) % 4, (1 - yl) * 4 + (x + 2) % 4]
    lo, hi = pl.ds(0, 2), pl.ds(2, 2)

    def row_copy(k, blk, part, to):
        v = R.at[blk] if part is None else R.at[blk, part]
        return send(OWN.at[0] if blk is order[0] else v, v, row_s, row_r.at[k], (r, to))

    row = [
        row_copy(0, order[0], None, across), row_copy(1, order[0], None, ahead), row_copy(2, order[0], None, behind),
        row_copy(3, order[1], None, ahead), row_copy(4, order[1], None, behind),
        row_copy(5, order[2], lo, ahead), row_copy(6, order[3], hi, behind),
        row_copy(7, order[4], lo, ahead), row_copy(8, order[5], hi, behind)]
    got = [
        row_copy(0, order[1], None, across), row_copy(1, order[2], None, ahead), row_copy(2, order[3], None, behind),
        row_copy(3, order[4], None, ahead), row_copy(4, order[5], None, behind),
        row_copy(5, order[6], lo, ahead), row_copy(6, order[6], hi, behind),
        row_copy(7, order[7], lo, ahead), row_copy(8, order[7], hi, behind)]

    mine, other = z // 2, 1 - z // 2
    below, above = ((z + 3) % 4) // 2, ((z + 1) % 4) // 2
    E, U, W = opts.get("parts", ((1, 4, 5, 7), (0, 3), (2, 6)))
    UW = U + W

    def move(src, dst, way, n, to): return send(src, dst, col_s.at[way], col_r.at[way, n], to)
    def r_block(k): return OWN.at[0] if k == 0 else R.at[order[k]]
    def r_copy(k, way): return send(r_block(k), C.at[mine, order[k]], col_s.at[way], col_r.at[way, k], ((up, down)[way], c))
    def c_copy(k, s, way, part=None):
        v = C.at[s, order[k]] if part is None else C.at[s, order[k], part]
        return move(v, v, way, k, ((up, down)[way], c))
    def cross(src, s, blk, n): return send(src, C.at[s, blk], col_s.at[2], mir_r.at[n], (mirror, c))
    def hold(_k):
        @pl.when(aside)
        def _():
            held.start()
    held = send(OWN.at[0], C.at[mine, c], hold_s, mir_r.at[x], (mirror, r % 8))
    def to_twin(src, s, blk): return send(src, C.at[s, blk], core_s, core_r, (twin, c))
    def own(k): return pltpu.make_async_copy(r_block(k), C.at[mine, order[k]], own_s.at[k])

    def col_source(k):
        @pl.when(source)
        def _():
            if k > 5:
                row_last(k)
            r_copy(k, 0).start(); r_copy(k, 1).start()
            own(k).start()
            to_twin(r_block(k), mine, order[k]).start()

    def row_step(k):
        if k == 1:
            got[0].wait_recv(); row[3].start(); row[4].start()
        elif k == 2:
            got[1].wait_recv(); row[5].start()
        elif k == 3:
            got[2].wait_recv(); row[6].start()
        elif k == 4:
            got[3].wait_recv(); row[7].start()
        elif k == 5:
            got[4].wait_recv(); row[8].start()
    def row_last(k):
        n = 2 * k - 7
        got[n].wait_recv(); got[n + 1].wait_recv()

    def row_rest(_k):
        for k in (6, 7):
            if do_col:
                @pl.when(no(source))
                def _():
                    row_last(k)
            else:
                row_last(k)

    def col_odd(k):
        @pl.when(odd)
        def _():
            for s, way, part, marks in ((below, 0, lo, U), (above, 1, hi, W)):
                c_copy(k, s, way).wait_recv()
                if k in marks:
                    cross(C.at[s, order[k]], s, order[k], UW.index(k)).start()
                c_copy(k, s, way, part).start()
                to_twin(C.at[s, order[k]], s, order[k]).start()

    def col_last(k):
        @pl.when(source)
        def _():
            c_copy(k, other, 0, lo).wait_recv(); c_copy(k, other, 1, hi).wait_recv()
            to_twin(C.at[other, order[k]], other, order[k]).start()

    def pick(flag, a, b): return jnp.where(flag, a, b)
    def far_own(i): return pick(even, mine, below if i < 2 else above), pick(even, order[E[i]], order[UW[i]])
    def far_down(i): return pick(even, other if i < 2 else mine, below), pick(even, order[UW[i]], order[E[i]])
    def far_up(i): return pick(even, mine if i < 2 else other, above), pick(even, order[UW[i]], order[E[i]])
    def far_next(i): return pick(even, other, above if i < 2 else below), far_own(i)[1]
    def far_copy(at, way, n, part=None):
        v = C.at[at[0], at[1]] if part is None else C.at[at[0], at[1], part]
        return move(v, v, way, n, ((up, down)[way], c))

    def far_first(i):
        @pl.when(far)
        def _():
            s, blk = far_own(i)
            cross(C.at[s, blk], s, blk, pick(even, blk % 4, i)).wait_recv()
            far_copy((s, blk), 0, i).start(); far_copy((s, blk), 1, i).start()
            to_twin(C.at[s, blk], s, blk).start()

    def far_pass(i):
        @pl.when(far)
        def _():
            for at, way, part in ((far_down(i), 0, lo), (far_up(i), 1, hi)):
                far_copy(at, way, i).wait_recv()
                far_copy(at, way, 4 + i, part).start()
                to_twin(C.at[at[0], at[1]], *at).start()

    def far_last(i):
        @pl.when(far)
        def _():
            at = far_next(i)
            far_copy(at, 0, 4 + i, lo).wait_recv(); far_copy(at, 1, 4 + i, hi).wait_recv()
            to_twin(C.at[at[0], at[1]], *at).start()

    def some(n, ss, part=None): return send(C.at[0, pl.ds(0, n)], C.at[0, pl.ds(0, n)], ss, core_r, (twin, c))

    def col_end():
        @pl.when(source)
        def _():
            some(8, col_s.at[0]).wait_send(); some(8, col_s.at[1]).wait_send()
            for k in range(8):
                own(k).wait()
        @pl.when(odd)
        def _():
            some(4, col_s.at[0]).wait_send(); some(4, col_s.at[1]).wait_send()
        @pl.when(far)
        def _():
            some(6, col_s.at[0]).wait_send(); some(6, col_s.at[1]).wait_send()
        @pl.when(odd)
        def _():
            some(4, col_s.at[2]).wait_send()
        @pl.when(aside)
        def _():
            held.wait_send()
        @pl.when(active)
        def _():
            send(C, C, core_s, core_r, (twin, c)).wait_send()
        @pl.when(no(active))
        def _():
            send(C, C, core_s, core_r, (twin, c)).wait_recv()

    ny = opts.get("ny", NY)
    first, rest = pl.ds(0, ny), pl.ds(ny, 4 - ny)
    targets = [(r + 8 - t) % 8 for t in range(3)]
    near_any = (targets[0] // 4 == yl) | (targets[1] // 4 == yl) | (targets[2] // 4 == yl)
    far_any = (targets[0] // 4 != yl) | (targets[1] // 4 != yl) | (targets[2] // 4 != yl)
    def left_near(t): return send(OWN.at[1], L.at[c], left_s.at[t], left_r.at[c], (r, targets[t]))
    def left_far(t): return send(OWN.at[1, rest], L.at[c, rest], left_s.at[t], left_r.at[c], (r, targets[t]))
    def left_over(): return send(OWN.at[1, first], L.at[c, first], over_s, over_r, (r, across))
    def left_on(t): return send(L.at[across, first], L.at[across, first], on_s.at[t], on_r.at[across], (r, targets[t]))
    def left_start(n):
        if n == 0 and ny:
            @pl.when(far_any)
            def _():
                left_over().start()
        for t, to in enumerate(targets):
            if n == 1:
                @pl.when((to != c) & (to // 4 == yl))
                def _():
                    left_near(t).start()
            if n == 2:
                @pl.when(to // 4 != yl)
                def _():
                    left_far(t).start()
    def left_turn(_k):
        if ny:
            @pl.when(near_any)
            def _():
                send(L.at[across, first], L.at[across, first], over_s, over_r, (r, across)).wait_recv()
            for t, to in enumerate(targets):
                @pl.when((to != c) & (to // 4 == yl))
                def _():
                    left_on(t).start()
    def left_end():
        if ny:
            @pl.when(far_any)
            def _():
                left_over().wait_send()
        for t, to in enumerate(targets):
            @pl.when((to != c) & (to // 4 == yl))
            def _():
                left_near(t).wait_send()
                if ny:
                    left_on(t).wait_send()
            @pl.when(to // 4 != yl)
            def _():
                left_far(t).wait_send()
    def left_got(k):
        blk = order[k]
        if k in (0,):
            return
        if k in (2, 3, 6):
            send(L.at[blk], L.at[blk], over_s, left_r.at[blk], (r, across)).wait_recv()
        else:
            send(L.at[blk, rest], L.at[blk, rest], over_s, left_r.at[blk], (r, across)).wait_recv()
            if ny and k != 1:
                send(L.at[blk, first], L.at[blk, first], over_s, on_r.at[blk], (r, across)).wait_recv()
    def l_twin(k): return send(OWN.at[1] if k == 0 else L.at[order[k]], J.at[order[k]], twin_s, twin_r, (twin, c))
    def j_twin(k): return send(J.at[order[k]], J.at[order[k]], twin_s, twin_r, (twin, c))
    def left_step(k):
        @pl.when(gap <= 2)
        def _():
            left_got(k)
        @pl.when((gap == 0) & (core == 0))
        def _():
            l_twin(k).start()

    goal = jnp.where(yh == 0, r, r + 12) % 8
    same = goal // 4 == yl
    lift = send(OWN.at[1], ZB, lift_s, lift_r, (up, c))
    def lift_start(_k):
        @pl.when(yh == 1)
        def _():
            lift.start()
    def part_from(src):
        return (send(src, XJ.at[x], next_s, relay_r.at[x], (mirror, (1 - goal // 4) * 4 + goal % 4)),
                send(src, J.at[c], next_s, next_r.at[c], (mirror, goal)))
    def part_start(k):
        @pl.when(yh == k)
        def _():
            if k == 1:
                lift.wait_recv()
            by, direct = part_from(ZB if k == 1 else OWN.at[1])
            @pl.when(same)
            def _():
                by.start()
            @pl.when(no(same))
            def _():
                direct.start()
    def relay(j): return send(XJ.at[j], J.at[(1 - yl) * 4 + j], relay_s, next_r.at[(1 - yl) * 4 + j], (r, across))
    def relay_step(j):
        @pl.when(hand)
        def _():
            send(XJ.at[j], XJ.at[j], relay_s, relay_r.at[j], (r, across)).wait_recv()
            relay(j).start()
    def next_step(k):
        @pl.when(gap == 2)
        def _():
            send(J.at[order[k]], J.at[order[k]], relay_s, next_r.at[order[k]], (r, across)).wait_recv()
        @pl.when((gap == 2) & (core == 1))
        def _():
            j_twin(k).start()
    def next_end():
        part_from(OWN.at[1])[1].wait_send()
        @pl.when(yh == 1)
        def _():
            lift.wait_send()
        @pl.when(hand)
        def _():
            send(XJ, XJ, relay_s, lift_r, (r, across)).wait_send()
        @pl.when(((gap == 0) & (core == 0)) | ((gap == 2) & (core == 1)))
        def _():
            send(J, J, twin_s, twin_r, (twin, c)).wait_send()
        @pl.when(gap == 1)
        def _():
            send(J, J, twin_s, twin_r, (twin, c)).wait_recv()

    do_col, do_left = opts.get("col", True), opts.get("left", True)
    for cp in row[:3]:
        cp.start()
    steps = dict(r=row_step, q=row_rest)
    if do_col:
        steps.update(s=col_source, M=hold, o=col_odd, e=col_last, c=far_first, d=far_pass, h=far_last)
    if do_left:
        steps.update(S=left_start, T=left_turn, l=left_step, n=next_step, Z=lift_start, J=part_start, x=relay_step)
    words = opts.get("order", ORDER)
    for word in (words.split() if isinstance(words, str) else words):
        if word[0] in steps:
            steps[word[0]](int(word[1:]))
    send(R.at[pl.ds(0, 7)], R.at[pl.ds(0, 7)], row_s, lift_r, (twin, c)).wait_send()
    for cp in keep:
        cp.wait()
    if do_left:
        left_end()
        next_end()
    if do_col:
        col_end()


bf = jnp.bfloat16
def D(*s): return pltpu.SemaphoreType.DMA(s)
SCRATCH = [pltpu.VMEM((4, 4, 128, 256), bf), pltpu.VMEM((4, 128, 256), bf), pltpu.VMEM((2, 4, 128, 256), bf),
           pltpu.VMEM((2, 4, 128, 256), bf), pltpu.SMEM((1, 4), jnp.int32), D(3),
           D(), D(9), D(3), D(2, 8), D(4), D(), D(),
           D(3), D(8), D(), D(8), D(), D(4), D(), D(), D(), D(), D(8), D(2), D(), D(), D(3), D(8), D()]
PANELS = [(8, 4, 128, 256), (2, 8, 4, 128, 256), (8, 4, 128, 256), (8, 4, 128, 256)]


def gather(panel_left, panel_right, panel_ranks, opts={}):
    V = pl.BlockSpec(memory_space=pltpu.VMEM)
    return pl.pallas_call(
        functools.partial(gather_kernel, opts=opts),
        out_shape=tuple(jax.ShapeDtypeStruct(s, bf) for s in PANELS),
        in_specs=[pl.BlockSpec(memory_space=pltpu.HBM)] * 3,
        out_specs=(pl.BlockSpec(memory_space=pl.ANY),) * 4,
        scratch_shapes=SCRATCH,
        compiler_params=pltpu.CompilerParams(collective_id=0, has_side_effects=True, vmem_limit_bytes=8 << 20),
        cost_estimate=pl.CostEstimate(flops=20_000_000_000, bytes_accessed=100_000_000, transcendentals=0),
        name="gather_panels",
    )(*(pltpu.with_memory_space_constraint(v, pltpu.HBM) for v in (panel_left, panel_right, panel_ranks)))


def update_kernel(R, C, L, J, mask_ref, tiles, core_out, dense_out,
                  flipped, cores, masked, dense, panels, lean, core_sem, dense_sem):
    r, c = lax.axis_index("row"), lax.axis_index("col")
    gap = (r + 8 - c) % 8
    has_tiles = gap <= 2
    shift = (r - gap - c) // 8

    def core_back(lj): return pltpu.make_async_copy(masked.at[:, lj], core_out.at[0, 0, :, lj], core_sem.at[lj])
    def dense_back(li): return pltpu.make_async_copy(dense.at[li], dense_out.at[0, 0, li], dense_sem.at[li])
    def zero_back(li): return pltpu.make_async_copy(dense.at[0], dense_out.at[0, 0, li], dense_sem.at[li])

    @pl.when(jnp.logical_not(has_tiles))
    def _():
        dense[0] = jnp.zeros((1024, 1024), jnp.bfloat16)
        for li in range(4):
            zero_back(li).start()

    for li in range(4):
        flipped[li] = R[:, li].reshape(1024, 256).T
    for lj in range(8):
        first = lj // 2
        right_j = C[lj % 2, :, first].reshape(1024, 256)
        wide = jnp.dot(flipped[first:].reshape((4 - first) * 256, 1024), right_j, preferred_element_type=jnp.float32)
        wide = wide.astype(jnp.bfloat16).reshape(4 - first, 256, 256)
        for li in range(4):
            if li < first:
                masked[li, lj] = jnp.zeros((256, 256), jnp.bfloat16)
            else:
                cores[li, lj] = wide[li - first]
                keep = (li * 16 + r >= lj * 8 + c) & (mask_ref[0, 0, li, lj] == 0)
                masked[li, lj] = jnp.where(keep, wide[li - first], jnp.zeros((256, 256), jnp.bfloat16))
        core_back(lj).start()

    @pl.when(has_tiles)
    def _():
        for li in range(4):
            lj = 2 * li + shift
            there = (lj >= 0) & (mask_ref[0, 0, li, jnp.maximum(lj, 0)] > 0)
            lj = jnp.maximum(lj, 0)
            back = jnp.where(r < gap, 1, 0)
            lj_row = jnp.maximum(li - back, 0)
            lean[...] = jnp.dot(L[:, li].reshape(1024, 256), cores[li, lj], preferred_element_type=jnp.float32).astype(jnp.bfloat16)

            @pl.when(gap == 0)
            def _():
                panels[...] = L[:, li].reshape(1024, 256)

            @pl.when(gap > 0)
            def _():
                panels[...] = J[:, lj_row].reshape(1024, 256)
            for part in range(4):
                rows = pl.ds(part * 256, 256)
                change = lax.dot_general(lean[rows], panels[...], (((1,), (1,)), ((), ())), preferred_element_type=jnp.float32)
                new = (tiles[0, 0, li, rows].astype(jnp.float32) - change).astype(jnp.bfloat16)
                dense[li, rows] = jnp.where(there, new, jnp.zeros_like(new))
            dense_back(li).start()

    for lj in range(8):
        core_back(lj).wait()
    for li in range(4):
        dense_back(li).wait()


def update(R, C, L, J, dense_mask, dense_tiles, vm=pltpu.VMEM):
    bf = jnp.bfloat16
    V = pl.BlockSpec(memory_space=vm)
    A = pl.BlockSpec(memory_space=pl.ANY)
    return pl.pallas_call(
        update_kernel,
        out_shape=(jax.ShapeDtypeStruct((1, 1, 4, 8, 256, 256), bf), jax.ShapeDtypeStruct((1, 1, 4, 1024, 1024), bf)),
        in_specs=[V, V, V, V, pl.BlockSpec(memory_space=pltpu.SMEM), V],
        out_specs=(A, A),
        scratch_shapes=[pltpu.VMEM((4, 256, 1024), bf), pltpu.VMEM((4, 8, 256, 256), bf), pltpu.VMEM((4, 8, 256, 256), bf),
                        pltpu.VMEM((4, 1024, 1024), bf), pltpu.VMEM((1024, 256), bf), pltpu.VMEM((1024, 256), bf),
                        pltpu.SemaphoreType.DMA((8,)), pltpu.SemaphoreType.DMA((4,))],
        compiler_params=pltpu.CompilerParams(vmem_limit_bytes=24 << 20),
        cost_estimate=pl.CostEstimate(flops=6_000_000_000, bytes_accessed=20_000_000, transcendentals=0),
        name="update_tiles",
    )(R, C, L, J, dense_mask, dense_tiles)


def per_device(panel_left, panel_right, panel_ranks, dense_mask, dense_tiles):
    R, C, L, J = gather(panel_left, panel_right, panel_ranks)
    return update(R, C, L, J, dense_mask, dense_tiles)


def solution(mesh):
    placed = (
        P("row", None, "col", None),
        P("row", None, "col", None),
        P("row", None),
        P("row", "col", None, None),
        P("row", "col", None, None, None),
    )
    return jax.shard_map(
        per_device,
        mesh=mesh,
        in_specs=placed,
        out_specs=(P("row", "col", None, None, None, None), P("row", "col", None, None, None)),
        check_vma=False,
    )
```

```python
import functools
import jax, jax.numpy as jnp
from jax import lax
from jax.experimental import pallas as pl
from jax.experimental.pallas import tpu as pltpu
from jax.sharding import PartitionSpec as P
MESH = pl.DeviceIdType.MESH
NY = 2
ORDER = ["M0", "r0", "s0", "r2", "r3", "s2", "s3", "r1", "o0", "s6", "S0", "o2", "o3", "s1", "o6", "Z0", "c0", "c2", "r5", "r4", "s4", "o1", "J0", "d2", "s5", "S1", "J1", "c1", "d0", "S2", "s7", "x1", "d1", "c3", "x2", "h1", "x0", "o5", "o4", "h0", "x3", "l0", "h2", "o7", "T0", "e3", "d3", "h3", "e2", "e5", "e6", "e1", "e0", "e7", "e4", "q0", "t0", "F0", "A0", "B0", "l1", "l2", "l3", "A1", "B1", "n1", "n3", "l4", "l5", "l6", "l7", "A2", "B2", "n2", "n5", "n4", "A3", "B3", "n7", "n0", "n6"]


def gather_kernel(left_in, right_in, rank_in, mask_in, U_out, M_out, L, J, R, C,
                  U, M, flipped, XJ, ZB, OWN, raw, rank_ref, mask_ref, load_s, out_s,
                  row_s, row_r, col_s, col_r, mir_r, core_s, core_r,
                  left_s, left_r, next_s, next_r, relay_s, relay_r, lift_s, lift_r, twin_s, twin_r, own_s, keep_s, over_s, over_r, on_s, on_r, hold_s, *, opts):
    r, c = lax.axis_index("row"), lax.axis_index("col")
    z, yh, core = r // 4, (r // 2) % 2, r % 2
    yl, x = c // 4, c % 4
    ahead, behind = yl * 4 + (x + 1) % 4, yl * 4 + (x + 3) % 4
    across = (1 - yl) * 4 + x
    up = ((z + 1) % 4) * 4 + yh * 2 + core
    down = ((z + 3) % 4) * 4 + yh * 2 + core
    mirror = z * 4 + (1 - yh) * 2 + core
    twin = z * 4 + yh * 2 + 1 - core
    gap = (r + 8 - c) % 8
    no = jnp.logical_not

    loads = [pltpu.make_async_copy(rank_in, rank_ref, load_s.at[2]), pltpu.make_async_copy(mask_in, mask_ref, load_s.at[3]),
             pltpu.make_async_copy(right_in.at[0], raw.at[0], load_s.at[0]), pltpu.make_async_copy(left_in.at[0], raw.at[1], load_s.at[1])]
    for cp in loads:
        cp.start()

    hand = across == (r + 14) % 8
    active = core == x % 2
    even = z % 2 == yl
    home = yh == x // 2
    source = active & even & home
    odd = active & no(even) & home
    far = active & no(home)
    aside = (r % 8) // 4 != yl
    barrier = pltpu.get_barrier_semaphore()
    partners = [(r, (c + k) % 8) for k in range(1, 8)] + [(up, c), (down, c), (mirror, c), (twin, c)]
    for p in partners:
        pl.semaphore_signal(barrier, inc=1, device_id=p, device_id_type=MESH)

    @pl.when(far & even)
    def _():
        for j in range(4):
            pl.semaphore_signal(barrier, inc=1, device_id=(mirror, (1 - yl) * 4 + j), device_id_type=MESH)

    @pl.when((gap == 2) | hand)
    def _():
        for j in range(4):
            pl.semaphore_signal(barrier, inc=1, device_id=(mirror, (1 - yl) * 4 + j), device_id_type=MESH)
    for cp in loads:
        cp.wait()
    lane = lax.broadcasted_iota(jnp.int32, (128, 256), 1)
    for li in range(4):
        kept = lane < rank_ref[0, li]
        zero = jnp.zeros((128, 256), jnp.bfloat16)
        OWN[0, li] = jnp.where(kept, raw[0, li], zero)
        OWN[1, li] = jnp.where(kept, raw[1, li], zero)
    keep = [pltpu.make_async_copy(OWN.at[0], R.at[c], keep_s.at[0]), pltpu.make_async_copy(OWN.at[1], L.at[c], keep_s.at[1])]
    for cp in keep:
        cp.start()

    pl.semaphore_wait(barrier, len(partners) + 1 + jnp.where(aside, 1, 0))

    def send(src, dst, ss, rs, to):
        return pltpu.make_async_remote_copy(src_ref=src, dst_ref=dst, send_sem=ss, recv_sem=rs, device_id=to, device_id_type=MESH)

    order = [c, across, behind, ahead, (1 - yl) * 4 + (x + 3) % 4, (1 - yl) * 4 + (x + 1) % 4, yl * 4 + (x + 2) % 4, (1 - yl) * 4 + (x + 2) % 4]
    lo, hi = pl.ds(0, 2), pl.ds(2, 2)

    def row_copy(k, blk, part, to):
        v = R.at[blk] if part is None else R.at[blk, part]
        return send(OWN.at[0] if blk is order[0] else v, v, row_s, row_r.at[k], (r, to))

    row = [
        row_copy(0, order[0], None, across), row_copy(1, order[0], None, ahead), row_copy(2, order[0], None, behind),
        row_copy(3, order[1], None, ahead), row_copy(4, order[1], None, behind),
        row_copy(5, order[2], lo, ahead), row_copy(6, order[3], hi, behind),
        row_copy(7, order[4], lo, ahead), row_copy(8, order[5], hi, behind)]
    got = [
        row_copy(0, order[1], None, across), row_copy(1, order[2], None, ahead), row_copy(2, order[3], None, behind),
        row_copy(3, order[4], None, ahead), row_copy(4, order[5], None, behind),
        row_copy(5, order[6], lo, ahead), row_copy(6, order[6], hi, behind),
        row_copy(7, order[7], lo, ahead), row_copy(8, order[7], hi, behind)]

    mine, other = z // 2, 1 - z // 2
    below, above = ((z + 3) % 4) // 2, ((z + 1) % 4) // 2
    E, UP, DN = opts.get("parts", ((1, 4, 5, 7), (0, 3), (2, 6)))
    UW = UP + DN

    def move(src, dst, way, n, to): return send(src, dst, col_s.at[way], col_r.at[way, n], to)
    def r_block(k): return OWN.at[0] if k == 0 else R.at[order[k]]
    def r_copy(k, way): return send(r_block(k), C.at[mine, order[k]], col_s.at[way], col_r.at[way, k], ((up, down)[way], c))
    def c_copy(k, s, way, part=None):
        v = C.at[s, order[k]] if part is None else C.at[s, order[k], part]
        return move(v, v, way, k, ((up, down)[way], c))
    def cross(src, s, blk, n): return send(src, C.at[s, blk], col_s.at[2], mir_r.at[n], (mirror, c))
    def hold(_k):
        @pl.when(aside)
        def _():
            held.start()
    held = send(OWN.at[0], C.at[mine, c], hold_s, mir_r.at[x], (mirror, r % 8))
    def to_twin(src, s, blk): return send(src, C.at[s, blk], core_s, core_r, (twin, c))
    def own(k): return pltpu.make_async_copy(r_block(k), C.at[mine, order[k]], own_s.at[k])

    def col_source(k):
        @pl.when(source)
        def _():
            if k > 5:
                row_last(k)
            r_copy(k, 0).start(); r_copy(k, 1).start()
            own(k).start()
            to_twin(r_block(k), mine, order[k]).start()

    def row_step(k):
        if k == 1:
            got[0].wait_recv(); row[3].start(); row[4].start()
        elif k == 2:
            got[1].wait_recv(); row[5].start()
        elif k == 3:
            got[2].wait_recv(); row[6].start()
        elif k == 4:
            got[3].wait_recv(); row[7].start()
        elif k == 5:
            got[4].wait_recv(); row[8].start()
    def row_last(k):
        n = 2 * k - 7
        got[n].wait_recv(); got[n + 1].wait_recv()

    def row_rest(_k):
        for k in (6, 7):
            if do_col:
                @pl.when(no(source))
                def _():
                    row_last(k)
            else:
                row_last(k)

    def col_odd(k):
        @pl.when(odd)
        def _():
            for s, way, part, marks in ((below, 0, lo, UP), (above, 1, hi, DN)):
                c_copy(k, s, way).wait_recv()
                if k in marks:
                    cross(C.at[s, order[k]], s, order[k], UW.index(k)).start()
                c_copy(k, s, way, part).start()
                to_twin(C.at[s, order[k]], s, order[k]).start()

    def col_last(k):
        @pl.when(source)
        def _():
            c_copy(k, other, 0, lo).wait_recv(); c_copy(k, other, 1, hi).wait_recv()
            to_twin(C.at[other, order[k]], other, order[k]).start()

    def pick(flag, a, b): return jnp.where(flag, a, b)
    def far_own(i): return pick(even, mine, below if i < 2 else above), pick(even, order[E[i]], order[UW[i]])
    def far_down(i): return pick(even, other if i < 2 else mine, below), pick(even, order[UW[i]], order[E[i]])
    def far_up(i): return pick(even, mine if i < 2 else other, above), pick(even, order[UW[i]], order[E[i]])
    def far_next(i): return pick(even, other, above if i < 2 else below), far_own(i)[1]
    def far_copy(at, way, n, part=None):
        v = C.at[at[0], at[1]] if part is None else C.at[at[0], at[1], part]
        return move(v, v, way, n, ((up, down)[way], c))

    def far_first(i):
        @pl.when(far)
        def _():
            s, blk = far_own(i)
            cross(C.at[s, blk], s, blk, pick(even, blk % 4, i)).wait_recv()
            far_copy((s, blk), 0, i).start(); far_copy((s, blk), 1, i).start()
            to_twin(C.at[s, blk], s, blk).start()

    def far_pass(i):
        @pl.when(far)
        def _():
            for at, way, part in ((far_down(i), 0, lo), (far_up(i), 1, hi)):
                far_copy(at, way, i).wait_recv()
                far_copy(at, way, 4 + i, part).start()
                to_twin(C.at[at[0], at[1]], *at).start()

    def far_last(i):
        @pl.when(far)
        def _():
            at = far_next(i)
            far_copy(at, 0, 4 + i, lo).wait_recv(); far_copy(at, 1, 4 + i, hi).wait_recv()
            to_twin(C.at[at[0], at[1]], *at).start()

    def some(n, ss, part=None): return send(C.at[0, pl.ds(0, n)], C.at[0, pl.ds(0, n)], ss, core_r, (twin, c))

    def col_end():
        @pl.when(source)
        def _():
            some(8, col_s.at[0]).wait_send(); some(8, col_s.at[1]).wait_send()
        @pl.when(odd)
        def _():
            some(4, col_s.at[0]).wait_send(); some(4, col_s.at[1]).wait_send()
        @pl.when(far)
        def _():
            some(6, col_s.at[0]).wait_send(); some(6, col_s.at[1]).wait_send()
        @pl.when(odd)
        def _():
            some(4, col_s.at[2]).wait_send()
        @pl.when(aside)
        def _():
            held.wait_send()
        @pl.when(active)
        def _():
            send(C, C, core_s, core_r, (twin, c)).wait_send()

    ny = opts.get("ny", NY)
    first, rest = pl.ds(0, ny), pl.ds(ny, 4 - ny)
    targets = [(r + 8 - t) % 8 for t in range(3)]
    near_any = (targets[0] // 4 == yl) | (targets[1] // 4 == yl) | (targets[2] // 4 == yl)
    far_any = (targets[0] // 4 != yl) | (targets[1] // 4 != yl) | (targets[2] // 4 != yl)
    def left_near(t): return send(OWN.at[1], L.at[c], left_s.at[t], left_r.at[c], (r, targets[t]))
    def left_far(t): return send(OWN.at[1, rest], L.at[c, rest], left_s.at[t], left_r.at[c], (r, targets[t]))
    def left_over(): return send(OWN.at[1, first], L.at[c, first], over_s, over_r, (r, across))
    def left_on(t): return send(L.at[across, first], L.at[across, first], on_s.at[t], on_r.at[across], (r, targets[t]))
    def left_start(n):
        if n == 0 and ny:
            @pl.when(far_any)
            def _():
                left_over().start()
        for t, to in enumerate(targets):
            if n == 1:
                @pl.when((to != c) & (to // 4 == yl))
                def _():
                    left_near(t).start()
            if n == 2:
                @pl.when(to // 4 != yl)
                def _():
                    left_far(t).start()
    def left_turn(_k):
        if ny:
            @pl.when(near_any)
            def _():
                send(L.at[across, first], L.at[across, first], over_s, over_r, (r, across)).wait_recv()
            for t, to in enumerate(targets):
                @pl.when((to != c) & (to // 4 == yl))
                def _():
                    left_on(t).start()
    def left_end():
        if ny:
            @pl.when(far_any)
            def _():
                left_over().wait_send()
        for t, to in enumerate(targets):
            @pl.when((to != c) & (to // 4 == yl))
            def _():
                left_near(t).wait_send()
                if ny:
                    left_on(t).wait_send()
            @pl.when(to // 4 != yl)
            def _():
                left_far(t).wait_send()
    def left_got(k):
        blk = order[k]
        if k in (0,):
            return
        if k in (2, 3, 6):
            send(L.at[blk], L.at[blk], over_s, left_r.at[blk], (r, across)).wait_recv()
        else:
            send(L.at[blk, rest], L.at[blk, rest], over_s, left_r.at[blk], (r, across)).wait_recv()
            if ny and k != 1:
                send(L.at[blk, first], L.at[blk, first], over_s, on_r.at[blk], (r, across)).wait_recv()
    def l_twin(k): return send(OWN.at[1] if k == 0 else L.at[order[k]], J.at[order[k]], twin_s, twin_r, (twin, c))
    def j_twin(k): return send(J.at[order[k]], J.at[order[k]], twin_s, twin_r, (twin, c))
    def left_step(k):
        @pl.when(gap <= 2)
        def _():
            left_got(k)
        @pl.when((gap == 0) & (core == 0))
        def _():
            l_twin(k).start()

    goal = jnp.where(yh == 0, r, r + 12) % 8
    same = goal // 4 == yl
    lift = send(OWN.at[1], ZB, lift_s, lift_r, (up, c))
    def lift_start(_k):
        @pl.when(yh == 1)
        def _():
            lift.start()
    def part_from(src):
        return (send(src, XJ.at[x], next_s, relay_r.at[x], (mirror, (1 - goal // 4) * 4 + goal % 4)),
                send(src, J.at[c], next_s, next_r.at[c], (mirror, goal)))
    def part_start(k):
        @pl.when(yh == k)
        def _():
            if k == 1:
                lift.wait_recv()
            by, direct = part_from(ZB if k == 1 else OWN.at[1])
            @pl.when(same)
            def _():
                by.start()
            @pl.when(no(same))
            def _():
                direct.start()
    def relay(j): return send(XJ.at[j], J.at[(1 - yl) * 4 + j], relay_s, next_r.at[(1 - yl) * 4 + j], (r, across))
    def relay_step(j):
        @pl.when(hand)
        def _():
            send(XJ.at[j], XJ.at[j], relay_s, relay_r.at[j], (r, across)).wait_recv()
            relay(j).start()
    def next_step(k):
        @pl.when(gap == 2)
        def _():
            send(J.at[order[k]], J.at[order[k]], relay_s, next_r.at[order[k]], (r, across)).wait_recv()
        @pl.when((gap == 2) & (core == 1))
        def _():
            j_twin(k).start()
    def next_end():
        part_from(OWN.at[1])[1].wait_send()
        @pl.when(yh == 1)
        def _():
            lift.wait_send()
        @pl.when(hand)
        def _():
            send(XJ, XJ, relay_s, lift_r, (r, across)).wait_send()
        @pl.when(((gap == 0) & (core == 0)) | ((gap == 2) & (core == 1)))
        def _():
            send(J, J, twin_s, twin_r, (twin, c)).wait_send()
        @pl.when(gap == 1)
        def _():
            send(J, J, twin_s, twin_r, (twin, c)).wait_recv()

    shift = (r - gap - c) // 8
    has_tiles = gap <= 2
    def core_flip(_k):
        keep[0].wait()

        @pl.when(has_tiles)
        def _():
            for li in range(4):
                flipped[li] = R[:, li].reshape(1024, 256).T
    def core_copy(lj): return pltpu.make_async_copy(U.at[:, lj], U_out.at[0, 0, :, lj], out_s)
    def core_step(q, s):
        lj = 2 * q + s

        @pl.when(has_tiles)
        def _():
            right_j = C[s, :, q].reshape(1024, 256)
            wide = jnp.dot(flipped[q:].reshape((4 - q) * 256, 1024), right_j, preferred_element_type=jnp.float32)
            wide = wide.astype(jnp.bfloat16).reshape(4 - q, 256, 256)
            for li in range(q):
                U[li, lj] = jnp.zeros((256, 256), jnp.bfloat16)
            for li in range(q, 4):
                kept = (li * 16 + r >= lj * 8 + c) & (mask_ref[0, 0, li, lj] == 0)
                U[li, lj] = jnp.where(kept, wide[li - q], jnp.zeros((256, 256), jnp.bfloat16))

            @pl.when(shift == s)
            def _():
                M[q] = wide[0]
            if q < 3:
                @pl.when((shift == -1) & (s == 1))
                def _():
                    M[q + 1] = wide[1]
            core_copy(lj).start()
    def core_end():

        @pl.when(has_tiles)
        def _():
            picks = pltpu.make_async_copy(M, M_out, load_s.at[0])
            picks.start()
            pltpu.make_async_copy(U, U_out.at[0, 0], out_s).wait()
            picks.wait()
    def twin_wait(_k):
        @pl.when(source)
        def _():
            for k in range(8):
                own(k).wait()
        @pl.when(no(active))
        def _():
            send(C, C, core_s, core_r, (twin, c)).wait_recv()

    do_col, do_left = opts.get("col", True), opts.get("left", True)
    for cp in row[:3]:
        cp.start()
    steps = dict(r=row_step, q=row_rest)
    if do_col:
        steps.update(s=col_source, M=hold, o=col_odd, e=col_last, c=far_first, d=far_pass, h=far_last, t=twin_wait)
        steps.update(F=core_flip, A=lambda q: core_step(q, mine), B=lambda q: core_step(q, other))
    if do_left:
        steps.update(S=left_start, T=left_turn, l=left_step, n=next_step, Z=lift_start, J=part_start, x=relay_step)
    words = opts.get("order", ORDER)
    for word in (words.split() if isinstance(words, str) else words):
        if word[0] in steps:
            steps[word[0]](int(word[1:]))
    send(R.at[pl.ds(0, 7)], R.at[pl.ds(0, 7)], row_s, lift_r, (twin, c)).wait_send()
    keep[1].wait()
    if do_col:
        core_end()
    if do_left:
        left_end()
        next_end()
    if do_col:
        col_end()


bf = jnp.bfloat16
def D(*s): return pltpu.SemaphoreType.DMA(s)
B = (4, 128, 256)
SCRATCH = [pltpu.VMEM((4, 8, 256, 256), bf), pltpu.VMEM((4, 256, 256), bf),
           pltpu.VMEM((4, 256, 1024), bf), pltpu.VMEM((4,) + B, bf), pltpu.VMEM(B, bf), pltpu.VMEM((2,) + B, bf),
           pltpu.VMEM((2,) + B, bf), pltpu.SMEM((1, 4), jnp.int32), pltpu.SMEM((1, 1, 4, 8), jnp.int32), D(4), D(),
           D(), D(9), D(3), D(2, 8), D(4), D(), D(),
           D(3), D(8), D(), D(8), D(), D(4), D(), D(), D(), D(), D(8), D(2), D(), D(), D(3), D(8), D()]
OUTS = [(1, 1, 4, 8, 256, 256), (4, 256, 256), (8,) + B, (8,) + B, (8,) + B, (2, 8) + B]


def gather(panel_left, panel_right, panel_ranks, dense_mask, opts={}, vm=12):
    return pl.pallas_call(
        functools.partial(gather_kernel, opts=opts),
        out_shape=tuple(jax.ShapeDtypeStruct(s, bf) for s in OUTS[:4]) + tuple(pltpu.VMEM(s, bf) for s in OUTS[4:]),
        in_specs=[pl.BlockSpec(memory_space=pltpu.HBM)] * 4,
        out_specs=(pl.BlockSpec(memory_space=pl.ANY),) * 4 + (pl.BlockSpec(memory_space=pltpu.VMEM),) * 2,
        scratch_shapes=SCRATCH,
        compiler_params=pltpu.CompilerParams(collective_id=0, has_side_effects=True, vmem_limit_bytes=vm << 20),
        cost_estimate=pl.CostEstimate(flops=20_000_000_000, bytes_accessed=100_000_000, transcendentals=0),
        name="gather_cores",
    )(*(pltpu.with_memory_space_constraint(v, pltpu.HBM) for v in (panel_left, panel_right, panel_ranks, dense_mask)))


def update_kernel(U, M, L, J, R, C, mask_ref, tiles, core_out, dense_out,
                  dense, panels, lean, flipped, masked, core_sem, dense_sem):
    r, c = lax.axis_index("row"), lax.axis_index("col")
    gap = (r + 8 - c) % 8
    has_tiles = gap <= 2
    shift = (r - gap - c) // 8

    def dense_back(li): return pltpu.make_async_copy(dense.at[li], dense_out.at[0, 0, li], dense_sem.at[li])
    def zero_back(li): return pltpu.make_async_copy(dense.at[0], dense_out.at[0, 0, li], dense_sem.at[li])
    core_back = pltpu.make_async_copy(U, core_out, core_sem)

    @pl.when(jnp.logical_not(has_tiles))
    def _():
        dense[0] = jnp.zeros((1024, 1024), jnp.bfloat16)
        for li in range(4):
            zero_back(li).start()
        for li in range(4):
            flipped[li] = R[:, li].reshape(1024, 256).T
        for lj in range(8):
            first = lj // 2
            right_j = C[lj % 2, :, first].reshape(1024, 256)
            wide = jnp.dot(flipped[first:].reshape((4 - first) * 256, 1024), right_j, preferred_element_type=jnp.float32)
            wide = wide.astype(jnp.bfloat16).reshape(4 - first, 256, 256)
            for li in range(4):
                if li < first:
                    masked[li, lj] = jnp.zeros((256, 256), jnp.bfloat16)
                else:
                    kept = (li * 16 + r >= lj * 8 + c) & (mask_ref[0, 0, li, lj] == 0)
                    masked[li, lj] = jnp.where(kept, wide[li - first], jnp.zeros((256, 256), jnp.bfloat16))
            pltpu.make_async_copy(masked.at[:, lj], core_out.at[0, 0, :, lj], core_sem).start()

    @pl.when(has_tiles)
    def _():
        core_back.start()
        for li in range(4):
            lj = 2 * li + shift
            there = (lj >= 0) & (mask_ref[0, 0, li, jnp.maximum(lj, 0)] > 0)
            lj_row = jnp.maximum(li - jnp.where(r < gap, 1, 0), 0)
            lean[...] = jnp.dot(L[:, li].reshape(1024, 256), M[li], preferred_element_type=jnp.float32).astype(jnp.bfloat16)

            @pl.when(gap == 0)
            def _():
                panels[...] = L[:, li].reshape(1024, 256)

            @pl.when(gap > 0)
            def _():
                panels[...] = J[:, lj_row].reshape(1024, 256)
            for part in range(4):
                rows = pl.ds(part * 256, 256)
                change = lax.dot_general(lean[rows], panels[...], (((1,), (1,)), ((), ())), preferred_element_type=jnp.float32)
                new = (tiles[0, 0, li, rows].astype(jnp.float32) - change).astype(jnp.bfloat16)
                dense[li, rows] = jnp.where(there, new, jnp.zeros_like(new))
            dense_back(li).start()

    core_back.wait()
    for li in range(4):
        dense_back(li).wait()


def update(U, M, L, J, R, C, dense_mask, dense_tiles):
    V, A = pl.BlockSpec(memory_space=pltpu.VMEM), pl.BlockSpec(memory_space=pl.ANY)
    return pl.pallas_call(
        update_kernel,
        out_shape=(jax.ShapeDtypeStruct((1, 1, 4, 8, 256, 256), bf), jax.ShapeDtypeStruct((1, 1, 4, 1024, 1024), bf)),
        in_specs=[A, V, V, V, V, V, pl.BlockSpec(memory_space=pltpu.SMEM), V],
        out_specs=(A, A),
        scratch_shapes=[pltpu.VMEM((4, 1024, 1024), bf), pltpu.VMEM((1024, 256), bf), pltpu.VMEM((1024, 256), bf),
                        pltpu.VMEM((4, 256, 1024), bf), pltpu.VMEM((4, 8, 256, 256), bf), D(), D(4)],
        compiler_params=pltpu.CompilerParams(vmem_limit_bytes=20 << 20),
        cost_estimate=pl.CostEstimate(flops=3_000_000_000, bytes_accessed=20_000_000, transcendentals=0),
        name="update_tiles",
    )(U, M, L, J, *(pltpu.with_memory_space_constraint(v, pltpu.VMEM) for v in (R, C)), dense_mask, dense_tiles)


def per_device(panel_left, panel_right, panel_ranks, dense_mask, dense_tiles):
    U, M, L, J, R, C = gather(panel_left, panel_right, panel_ranks, dense_mask)
    return update(U, M, L, J, R, C, dense_mask, dense_tiles)


def solution(mesh):
    placed = (
        P("row", None, "col", None),
        P("row", None, "col", None),
        P("row", None),
        P("row", "col", None, None),
        P("row", "col", None, None, None),
    )
    return jax.shard_map(
        per_device,
        mesh=mesh,
        in_specs=placed,
        out_specs=(P("row", "col", None, None, None, None), P("row", "col", None, None, None)),
        check_vma=False,
    )
```

```python
import functools
import jax, jax.numpy as jnp
from jax import lax
from jax.experimental import pallas as pl
from jax.experimental.pallas import tpu as pltpu
from jax.sharding import PartitionSpec as P
MESH = pl.DeviceIdType.MESH
NY = 2
ORDER = [
    "Z0", "M0", "r0", "s0", "r2", "r3", "s2", "s3", "o0", "S0", "r1", "o2", "s6", "o3", "s1", "o6",
    "c2", "r5", "r4", "o1", "s4", "J0", "c0", "d2", "s5", "S1", "J1", "c1", "d0", "S2", "s7", "x1",
    "d1", "c3", "T0", "x2", "h1", "x0", "o4", "h0", "x3", "d3", "o5", "h2", "o7", "e5", "e3", "h3",
    "e2", "e6", "e1", "e0", "e7", "e4", "q0", "t0", "F0", "B0", "B1", "A0", "l1", "l0", "l3", "l2",
    "l6", "A3", "l5", "A1", "n3", "A2", "n5", "n1", "B2", "n4", "n7", "B3", "n0", "n2", "l4", "l7",
    "n6",
]


def gather_kernel(left_in, right_in, rank_in, mask_in, U_out, M_out, L, J, R, C,
                  U, M, flipped, XJ, ZB, OWN, raw, rank_ref, mask_ref, load_s, out_s,
                  row_s, row_r, col_s, col_r, mir_r, core_s, core_r,
                  left_s, left_r, next_s, next_r, relay_s, relay_r, lift_s, lift_r, twin_s, twin_r, own_s, keep_s, over_s, over_r, on_s, on_r, hold_s, *, opts):
    r, c = lax.axis_index("row"), lax.axis_index("col")
    z, yh, core = r // 4, (r // 2) % 2, r % 2
    yl, x = c // 4, c % 4
    ahead, behind = yl * 4 + (x + 1) % 4, yl * 4 + (x + 3) % 4
    across = (1 - yl) * 4 + x
    up = ((z + 1) % 4) * 4 + yh * 2 + core
    down = ((z + 3) % 4) * 4 + yh * 2 + core
    mirror = z * 4 + (1 - yh) * 2 + core
    twin = z * 4 + yh * 2 + 1 - core
    gap = (r + 8 - c) % 8
    no = jnp.logical_not

    loads = [pltpu.make_async_copy(rank_in, rank_ref, load_s.at[2]), pltpu.make_async_copy(mask_in, mask_ref, load_s.at[3]),
             pltpu.make_async_copy(right_in.at[0], raw.at[0], load_s.at[0]), pltpu.make_async_copy(left_in.at[0], raw.at[1], load_s.at[1])]
    for cp in loads:
        cp.start()

    hand = across == (r + 14) % 8
    active = core == x % 2
    even = z % 2 == yl
    home = yh == x // 2
    source = active & even & home
    odd = active & no(even) & home
    far = active & no(home)
    aside = (r % 8) // 4 != yl
    barrier = pltpu.get_barrier_semaphore()
    partners = [(r, (c + k) % 8) for k in range(1, 8)] + [(up, c), (down, c), (mirror, c), (twin, c)]
    for p in partners:
        pl.semaphore_signal(barrier, inc=1, device_id=p, device_id_type=MESH)

    @pl.when(far & even)
    def _():
        for j in range(4):
            pl.semaphore_signal(barrier, inc=1, device_id=(mirror, (1 - yl) * 4 + j), device_id_type=MESH)

    @pl.when((gap == 2) | hand)
    def _():
        for j in range(4):
            pl.semaphore_signal(barrier, inc=1, device_id=(mirror, (1 - yl) * 4 + j), device_id_type=MESH)
    for cp in loads:
        cp.wait()
    lane = lax.broadcasted_iota(jnp.int32, (128, 256), 1)
    for li in range(4):
        kept = lane < rank_ref[0, li]
        zero = jnp.zeros((128, 256), jnp.bfloat16)
        OWN[0, li] = jnp.where(kept, raw[0, li], zero)
        OWN[1, li] = jnp.where(kept, raw[1, li], zero)
    keep = [pltpu.make_async_copy(OWN.at[0], R.at[c], keep_s.at[0]), pltpu.make_async_copy(OWN.at[1], L.at[c], keep_s.at[1])]
    for cp in keep:
        cp.start()

    pl.semaphore_wait(barrier, len(partners) + 1 + jnp.where(aside, 1, 0))

    def send(src, dst, ss, rs, to):
        return pltpu.make_async_remote_copy(src_ref=src, dst_ref=dst, send_sem=ss, recv_sem=rs, device_id=to, device_id_type=MESH)

    order = [c, across, behind, ahead, (1 - yl) * 4 + (x + 3) % 4, (1 - yl) * 4 + (x + 1) % 4, yl * 4 + (x + 2) % 4, (1 - yl) * 4 + (x + 2) % 4]
    lo, hi = pl.ds(0, 2), pl.ds(2, 2)

    def row_copy(k, blk, part, to):
        v = R.at[blk] if part is None else R.at[blk, part]
        return send(OWN.at[0] if blk is order[0] else v, v, row_s, row_r.at[k], (r, to))

    row = [
        row_copy(0, order[0], None, across), row_copy(1, order[0], None, ahead), row_copy(2, order[0], None, behind),
        row_copy(3, order[1], None, ahead), row_copy(4, order[1], None, behind),
        row_copy(5, order[2], lo, ahead), row_copy(6, order[3], hi, behind),
        row_copy(7, order[4], lo, ahead), row_copy(8, order[5], hi, behind)]
    got = [
        row_copy(0, order[1], None, across), row_copy(1, order[2], None, ahead), row_copy(2, order[3], None, behind),
        row_copy(3, order[4], None, ahead), row_copy(4, order[5], None, behind),
        row_copy(5, order[6], lo, ahead), row_copy(6, order[6], hi, behind),
        row_copy(7, order[7], lo, ahead), row_copy(8, order[7], hi, behind)]

    mine, other = z // 2, 1 - z // 2
    below, above = ((z + 3) % 4) // 2, ((z + 1) % 4) // 2
    E, UP, DN = opts.get("parts", ((1, 4, 5, 7), (0, 3), (2, 6)))
    UW = UP + DN

    def move(src, dst, way, n, to): return send(src, dst, col_s.at[way], col_r.at[way, n], to)
    def r_block(k): return OWN.at[0] if k == 0 else R.at[order[k]]
    def r_copy(k, way): return send(r_block(k), C.at[mine, order[k]], col_s.at[way], col_r.at[way, k], ((up, down)[way], c))
    def c_copy(k, s, way, part=None):
        v = C.at[s, order[k]] if part is None else C.at[s, order[k], part]
        return move(v, v, way, k, ((up, down)[way], c))
    def cross(src, s, blk, n): return send(src, C.at[s, blk], col_s.at[2], mir_r.at[n], (mirror, c))
    def hold(_k):
        @pl.when(aside)
        def _():
            held.start()
    held = send(OWN.at[0], C.at[mine, c], hold_s, mir_r.at[x], (mirror, r % 8))
    def to_twin(src, s, blk): return send(src, C.at[s, blk], core_s, core_r, (twin, c))
    def own(k): return pltpu.make_async_copy(r_block(k), C.at[mine, order[k]], own_s.at[k])

    def col_source(k):
        @pl.when(source)
        def _():
            if k > 5:
                row_last(k)
            r_copy(k, 0).start(); r_copy(k, 1).start()
            own(k).start()
            to_twin(r_block(k), mine, order[k]).start()

    def row_step(k):
        if k == 1:
            got[0].wait_recv(); row[3].start(); row[4].start()
        elif k == 2:
            got[1].wait_recv(); row[5].start()
        elif k == 3:
            got[2].wait_recv(); row[6].start()
        elif k == 4:
            got[3].wait_recv(); row[7].start()
        elif k == 5:
            got[4].wait_recv(); row[8].start()
    def row_last(k):
        n = 2 * k - 7
        got[n].wait_recv(); got[n + 1].wait_recv()

    def row_rest(_k):
        for k in (6, 7):
            if do_col:
                @pl.when(no(source))
                def _():
                    row_last(k)
            else:
                row_last(k)

    def col_odd(k):
        @pl.when(odd)
        def _():
            for s, way, part, marks in ((below, 0, lo, UP), (above, 1, hi, DN)):
                c_copy(k, s, way).wait_recv()
                if k in marks:
                    cross(C.at[s, order[k]], s, order[k], UW.index(k)).start()
                c_copy(k, s, way, part).start()
                to_twin(C.at[s, order[k]], s, order[k]).start()

    def col_last(k):
        @pl.when(source)
        def _():
            c_copy(k, other, 0, lo).wait_recv(); c_copy(k, other, 1, hi).wait_recv()
            to_twin(C.at[other, order[k]], other, order[k]).start()

    def pick(flag, a, b): return jnp.where(flag, a, b)
    def far_own(i): return pick(even, mine, below if i < 2 else above), pick(even, order[E[i]], order[UW[i]])
    def far_down(i): return pick(even, other if i < 2 else mine, below), pick(even, order[UW[i]], order[E[i]])
    def far_up(i): return pick(even, mine if i < 2 else other, above), pick(even, order[UW[i]], order[E[i]])
    def far_next(i): return pick(even, other, above if i < 2 else below), far_own(i)[1]
    def far_copy(at, way, n, part=None):
        v = C.at[at[0], at[1]] if part is None else C.at[at[0], at[1], part]
        return move(v, v, way, n, ((up, down)[way], c))

    def far_first(i):
        @pl.when(far)
        def _():
            s, blk = far_own(i)
            cross(C.at[s, blk], s, blk, pick(even, blk % 4, i)).wait_recv()
            far_copy((s, blk), 0, i).start(); far_copy((s, blk), 1, i).start()
            to_twin(C.at[s, blk], s, blk).start()

    def far_pass(i):
        @pl.when(far)
        def _():
            for at, way, part in ((far_down(i), 0, lo), (far_up(i), 1, hi)):
                far_copy(at, way, i).wait_recv()
                far_copy(at, way, 4 + i, part).start()
                to_twin(C.at[at[0], at[1]], *at).start()

    def far_last(i):
        @pl.when(far)
        def _():
            at = far_next(i)
            far_copy(at, 0, 4 + i, lo).wait_recv(); far_copy(at, 1, 4 + i, hi).wait_recv()
            to_twin(C.at[at[0], at[1]], *at).start()

    def some(n, ss, part=None): return send(C.at[0, pl.ds(0, n)], C.at[0, pl.ds(0, n)], ss, core_r, (twin, c))

    def col_end():
        @pl.when(source)
        def _():
            some(8, col_s.at[0]).wait_send(); some(8, col_s.at[1]).wait_send()
        @pl.when(odd)
        def _():
            some(4, col_s.at[0]).wait_send(); some(4, col_s.at[1]).wait_send()
        @pl.when(far)
        def _():
            some(6, col_s.at[0]).wait_send(); some(6, col_s.at[1]).wait_send()
        @pl.when(odd)
        def _():
            some(4, col_s.at[2]).wait_send()
        @pl.when(aside)
        def _():
            held.wait_send()
        @pl.when(active)
        def _():
            send(C, C, core_s, core_r, (twin, c)).wait_send()

    ny = opts.get("ny", NY)
    first, rest = pl.ds(0, ny), pl.ds(ny, 4 - ny)
    targets = [(r + 8 - t) % 8 for t in range(3)]
    near_any = (targets[0] // 4 == yl) | (targets[1] // 4 == yl) | (targets[2] // 4 == yl)
    far_any = (targets[0] // 4 != yl) | (targets[1] // 4 != yl) | (targets[2] // 4 != yl)
    def left_near(t): return send(OWN.at[1], L.at[c], left_s.at[t], left_r.at[c], (r, targets[t]))
    def left_far(t): return send(OWN.at[1, rest], L.at[c, rest], left_s.at[t], left_r.at[c], (r, targets[t]))
    def left_over(): return send(OWN.at[1, first], L.at[c, first], over_s, over_r, (r, across))
    def left_on(t): return send(L.at[across, first], L.at[across, first], on_s.at[t], on_r.at[across], (r, targets[t]))
    def left_start(n):
        if n == 0 and ny:
            @pl.when(far_any)
            def _():
                left_over().start()
        for t, to in enumerate(targets):
            if n == 1:
                @pl.when((to != c) & (to // 4 == yl))
                def _():
                    left_near(t).start()
            if n == 2:
                @pl.when(to // 4 != yl)
                def _():
                    left_far(t).start()
    def left_turn(_k):
        if ny:
            @pl.when(near_any)
            def _():
                send(L.at[across, first], L.at[across, first], over_s, over_r, (r, across)).wait_recv()
            for t, to in enumerate(targets):
                @pl.when((to != c) & (to // 4 == yl))
                def _():
                    left_on(t).start()
    def left_end():
        if ny:
            @pl.when(far_any)
            def _():
                left_over().wait_send()
        for t, to in enumerate(targets):
            @pl.when((to != c) & (to // 4 == yl))
            def _():
                left_near(t).wait_send()
                if ny:
                    left_on(t).wait_send()
            @pl.when(to // 4 != yl)
            def _():
                left_far(t).wait_send()
    def left_got(k):
        blk = order[k]
        if k in (0,):
            return
        if k in (2, 3, 6):
            send(L.at[blk], L.at[blk], over_s, left_r.at[blk], (r, across)).wait_recv()
        else:
            send(L.at[blk, rest], L.at[blk, rest], over_s, left_r.at[blk], (r, across)).wait_recv()
            if ny and k != 1:
                send(L.at[blk, first], L.at[blk, first], over_s, on_r.at[blk], (r, across)).wait_recv()
    def l_twin(k): return send(OWN.at[1] if k == 0 else L.at[order[k]], J.at[order[k]], twin_s, twin_r, (twin, c))
    def j_twin(k): return send(J.at[order[k]], J.at[order[k]], twin_s, twin_r, (twin, c))
    def left_step(k):
        @pl.when(gap <= 2)
        def _():
            left_got(k)
        @pl.when((gap == 0) & (core == 0))
        def _():
            l_twin(k).start()

    goal = jnp.where(yh == 0, r, r + 12) % 8
    same = goal // 4 == yl
    lift = send(OWN.at[1], ZB, lift_s, lift_r, (up, c))
    def lift_start(_k):
        @pl.when(yh == 1)
        def _():
            lift.start()
    def part_from(src):
        return (send(src, XJ.at[x], next_s, relay_r.at[x], (mirror, (1 - goal // 4) * 4 + goal % 4)),
                send(src, J.at[c], next_s, next_r.at[c], (mirror, goal)))
    def part_start(k):
        @pl.when(yh == k)
        def _():
            if k == 1:
                lift.wait_recv()
            by, direct = part_from(ZB if k == 1 else OWN.at[1])
            @pl.when(same)
            def _():
                by.start()
            @pl.when(no(same))
            def _():
                direct.start()
    def relay(j): return send(XJ.at[j], J.at[(1 - yl) * 4 + j], relay_s, next_r.at[(1 - yl) * 4 + j], (r, across))
    def relay_step(j):
        @pl.when(hand)
        def _():
            send(XJ.at[j], XJ.at[j], relay_s, relay_r.at[j], (r, across)).wait_recv()
            relay(j).start()
    def next_step(k):
        @pl.when(gap == 2)
        def _():
            send(J.at[order[k]], J.at[order[k]], relay_s, next_r.at[order[k]], (r, across)).wait_recv()
        @pl.when((gap == 2) & (core == 1))
        def _():
            j_twin(k).start()
    def next_end():
        part_from(OWN.at[1])[1].wait_send()
        @pl.when(yh == 1)
        def _():
            lift.wait_send()
        @pl.when(hand)
        def _():
            send(XJ, XJ, relay_s, lift_r, (r, across)).wait_send()
        @pl.when(((gap == 0) & (core == 0)) | ((gap == 2) & (core == 1)))
        def _():
            send(J, J, twin_s, twin_r, (twin, c)).wait_send()
        @pl.when(gap == 1)
        def _():
            send(J, J, twin_s, twin_r, (twin, c)).wait_recv()

    shift = (r - gap - c) // 8
    has_tiles = gap <= 2
    def core_flip(_k):
        keep[0].wait()

        @pl.when(has_tiles)
        def _():
            for li in range(4):
                flipped[li] = R[:, li].reshape(1024, 256).T
    def core_copy(lj): return pltpu.make_async_copy(U.at[:, lj], U_out.at[0, 0, :, lj], out_s)
    def core_step(q, s):
        lj = 2 * q + s

        @pl.when(has_tiles)
        def _():
            right_j = C[s, :, q].reshape(1024, 256)
            wide = jnp.dot(flipped[q:].reshape((4 - q) * 256, 1024), right_j, preferred_element_type=jnp.float32)
            wide = wide.astype(jnp.bfloat16).reshape(4 - q, 256, 256)
            for li in range(q):
                U[li, lj] = jnp.zeros((256, 256), jnp.bfloat16)
            for li in range(q, 4):
                kept = (li * 16 + r >= lj * 8 + c) & (mask_ref[0, 0, li, lj] == 0)
                U[li, lj] = jnp.where(kept, wide[li - q], jnp.zeros((256, 256), jnp.bfloat16))

            @pl.when(shift == s)
            def _():
                M[q] = wide[0]
            if q < 3:
                @pl.when((shift == -1) & (s == 1))
                def _():
                    M[q + 1] = wide[1]
            core_copy(lj).start()
    def core_end():

        @pl.when(has_tiles)
        def _():
            picks = pltpu.make_async_copy(M, M_out, load_s.at[0])
            picks.start()
            pltpu.make_async_copy(U, U_out.at[0, 0], out_s).wait()
            picks.wait()
    def twin_wait(_k):
        @pl.when(source)
        def _():
            for k in range(8):
                own(k).wait()
        @pl.when(no(active))
        def _():
            send(C, C, core_s, core_r, (twin, c)).wait_recv()

    do_col, do_left = opts.get("col", True), opts.get("left", True)
    for cp in row[:3]:
        cp.start()
    steps = dict(r=row_step, q=row_rest)
    if do_col:
        steps.update(s=col_source, M=hold, o=col_odd, e=col_last, c=far_first, d=far_pass, h=far_last, t=twin_wait)
        steps.update(F=core_flip, A=lambda q: core_step(q, mine), B=lambda q: core_step(q, other))
    if do_left:
        steps.update(S=left_start, T=left_turn, l=left_step, n=next_step, Z=lift_start, J=part_start, x=relay_step)
    words = opts.get("order", ORDER)
    for word in (words.split() if isinstance(words, str) else words):
        if word[0] in steps:
            steps[word[0]](int(word[1:]))
    send(R.at[pl.ds(0, 7)], R.at[pl.ds(0, 7)], row_s, lift_r, (twin, c)).wait_send()
    keep[1].wait()
    if do_col:
        core_end()
    if do_left:
        left_end()
        next_end()
    if do_col:
        col_end()


bf = jnp.bfloat16
def D(*s): return pltpu.SemaphoreType.DMA(s)
B = (4, 128, 256)
SCRATCH = [pltpu.VMEM((4, 8, 256, 256), bf), pltpu.VMEM((4, 256, 256), bf),
           pltpu.VMEM((4, 256, 1024), bf), pltpu.VMEM((4,) + B, bf), pltpu.VMEM(B, bf), pltpu.VMEM((2,) + B, bf),
           pltpu.VMEM((2,) + B, bf), pltpu.SMEM((1, 4), jnp.int32), pltpu.SMEM((1, 1, 4, 8), jnp.int32), D(4), D(),
           D(), D(9), D(3), D(2, 8), D(4), D(), D(),
           D(3), D(8), D(), D(8), D(), D(4), D(), D(), D(), D(), D(8), D(2), D(), D(), D(3), D(8), D()]
OUTS = [(1, 1, 4, 8, 256, 256), (4, 256, 256), (8,) + B, (8,) + B, (8,) + B, (2, 8) + B]


def gather(panel_left, panel_right, panel_ranks, dense_mask, opts={}, vm=12):
    return pl.pallas_call(
        functools.partial(gather_kernel, opts=opts),
        out_shape=tuple(jax.ShapeDtypeStruct(s, bf) for s in OUTS[:4]) + tuple(pltpu.VMEM(s, bf) for s in OUTS[4:]),
        in_specs=[pl.BlockSpec(memory_space=pltpu.HBM)] * 4,
        out_specs=(pl.BlockSpec(memory_space=pl.ANY),) * 4 + (pl.BlockSpec(memory_space=pltpu.VMEM),) * 2,
        scratch_shapes=SCRATCH,
        compiler_params=pltpu.CompilerParams(collective_id=0, has_side_effects=True, vmem_limit_bytes=vm << 20),
        cost_estimate=pl.CostEstimate(flops=20_000_000_000, bytes_accessed=100_000_000, transcendentals=0),
        name="gather_cores",
    )(*(pltpu.with_memory_space_constraint(v, pltpu.HBM) for v in (panel_left, panel_right, panel_ranks, dense_mask)))


def update_kernel(U, M, L, J, R, C, mask_ref, tiles, core_out, dense_out,
                  dense, panels, lean, flipped, masked, core_sem, dense_sem):
    r, c = lax.axis_index("row"), lax.axis_index("col")
    gap = (r + 8 - c) % 8
    has_tiles = gap <= 2
    shift = (r - gap - c) // 8

    def dense_back(li): return pltpu.make_async_copy(dense.at[li], dense_out.at[0, 0, li], dense_sem.at[li])
    def zero_back(li): return pltpu.make_async_copy(dense.at[0], dense_out.at[0, 0, li], dense_sem.at[li])
    core_back = pltpu.make_async_copy(U, core_out, core_sem)

    @pl.when(jnp.logical_not(has_tiles))
    def _():
        dense[0] = jnp.zeros((1024, 1024), jnp.bfloat16)
        for li in range(4):
            zero_back(li).start()
        for li in range(4):
            flipped[li] = R[:, li].reshape(1024, 256).T
        for lj in range(8):
            first = lj // 2
            right_j = C[lj % 2, :, first].reshape(1024, 256)
            wide = jnp.dot(flipped[first:].reshape((4 - first) * 256, 1024), right_j, preferred_element_type=jnp.float32)
            wide = wide.astype(jnp.bfloat16).reshape(4 - first, 256, 256)
            for li in range(4):
                if li < first:
                    masked[li, lj] = jnp.zeros((256, 256), jnp.bfloat16)
                else:
                    kept = (li * 16 + r >= lj * 8 + c) & (mask_ref[0, 0, li, lj] == 0)
                    masked[li, lj] = jnp.where(kept, wide[li - first], jnp.zeros((256, 256), jnp.bfloat16))
            pltpu.make_async_copy(masked.at[:, lj], core_out.at[0, 0, :, lj], core_sem).start()

    @pl.when(has_tiles)
    def _():
        core_back.start()
        for li in range(4):
            lj = 2 * li + shift
            there = (lj >= 0) & (mask_ref[0, 0, li, jnp.maximum(lj, 0)] > 0)
            lj_row = jnp.maximum(li - jnp.where(r < gap, 1, 0), 0)
            lean[...] = jnp.dot(L[:, li].reshape(1024, 256), M[li], preferred_element_type=jnp.float32).astype(jnp.bfloat16)

            @pl.when(gap == 0)
            def _():
                panels[...] = L[:, li].reshape(1024, 256)

            @pl.when(gap > 0)
            def _():
                panels[...] = J[:, lj_row].reshape(1024, 256)
            for part in range(4):
                rows = pl.ds(part * 256, 256)
                change = lax.dot_general(lean[rows], panels[...], (((1,), (1,)), ((), ())), preferred_element_type=jnp.float32)
                new = (tiles[0, 0, li, rows].astype(jnp.float32) - change).astype(jnp.bfloat16)
                dense[li, rows] = jnp.where(there, new, jnp.zeros_like(new))
            dense_back(li).start()

    core_back.wait()
    for li in range(4):
        dense_back(li).wait()


def update(U, M, L, J, R, C, dense_mask, dense_tiles):
    V, A = pl.BlockSpec(memory_space=pltpu.VMEM), pl.BlockSpec(memory_space=pl.ANY)
    return pl.pallas_call(
        update_kernel,
        out_shape=(jax.ShapeDtypeStruct((1, 1, 4, 8, 256, 256), bf), jax.ShapeDtypeStruct((1, 1, 4, 1024, 1024), bf)),
        in_specs=[A, V, V, V, V, V, pl.BlockSpec(memory_space=pltpu.SMEM), V],
        out_specs=(A, A),
        scratch_shapes=[pltpu.VMEM((4, 1024, 1024), bf), pltpu.VMEM((1024, 256), bf), pltpu.VMEM((1024, 256), bf),
                        pltpu.VMEM((4, 256, 1024), bf), pltpu.VMEM((4, 8, 256, 256), bf), D(), D(4)],
        compiler_params=pltpu.CompilerParams(vmem_limit_bytes=20 << 20),
        cost_estimate=pl.CostEstimate(flops=3_000_000_000, bytes_accessed=20_000_000, transcendentals=0),
        name="update_tiles",
    )(U, M, L, J, *(pltpu.with_memory_space_constraint(v, pltpu.VMEM) for v in (R, C)), dense_mask, dense_tiles)


def per_device(panel_left, panel_right, panel_ranks, dense_mask, dense_tiles):
    U, M, L, J, R, C = gather(panel_left, panel_right, panel_ranks, dense_mask)
    return update(U, M, L, J, R, C, dense_mask, dense_tiles)


def solution(mesh):
    placed = (
        P("row", None, "col", None),
        P("row", None, "col", None),
        P("row", None),
        P("row", "col", None, None),
        P("row", "col", None, None, None),
    )
    return jax.shard_map(
        per_device,
        mesh=mesh,
        in_specs=placed,
        out_specs=(P("row", "col", None, None, None, None), P("row", "col", None, None, None)),
        check_vma=False,
    )
```

```python
import functools
import jax, jax.numpy as jnp
from jax import lax
from jax.experimental import pallas as pl
from jax.experimental.pallas import tpu as pltpu
from jax.sharding import PartitionSpec as P
MESH = pl.DeviceIdType.MESH
NY = 2
ORDER = [
    "Z0", "M0", "r0", "s0", "r2", "r3", "s2", "s3", "o0", "S0", "r1", "o2", "s6", "o3", "s1", "o6",
    "c2", "r5", "r4", "o1", "s4", "J0", "c0", "d2", "s5", "S1", "J1", "c1", "d0", "S2", "s7", "x1",
    "d1", "c3", "T0", "x2", "h1", "x0", "o4", "h0", "x3", "d3", "o5", "h2", "o7", "e5", "e3", "h3",
    "e2", "e6", "e1", "e0", "e7", "e4", "q0", "t0", "F0", "B0", "B1", "A0", "l1", "l0", "l3", "l2",
    "l6", "A3", "l5", "A1", "n3", "A2", "n5", "n1", "B2", "n4", "n7", "B3", "n0", "n2", "l4", "l7",
    "n6",
]


def gather_kernel(left_in, right_in, rank_in, mask_in, U_out, M_out, L, J, R, C,
                  U, M, flipped, XJ, ZB, OWN, raw, rank_ref, mask_ref, load_s, out_s,
                  row_s, row_r, col_s, col_r, mir_r, core_s, core_r,
                  left_s, left_r, next_s, next_r, relay_s, relay_r, lift_s, lift_r, twin_s, twin_r, own_s, keep_s, over_s, over_r, on_s, on_r, hold_s, *, opts):
    r, c = lax.axis_index("row"), lax.axis_index("col")
    z, yh, core = r // 4, (r // 2) % 2, r % 2
    yl, x = c // 4, c % 4
    ahead, behind = yl * 4 + (x + 1) % 4, yl * 4 + (x + 3) % 4
    across = (1 - yl) * 4 + x
    up = ((z + 1) % 4) * 4 + yh * 2 + core
    down = ((z + 3) % 4) * 4 + yh * 2 + core
    mirror = z * 4 + (1 - yh) * 2 + core
    twin = z * 4 + yh * 2 + 1 - core
    gap = (r + 8 - c) % 8
    no = jnp.logical_not

    loads = [pltpu.make_async_copy(rank_in, rank_ref, load_s.at[2]), pltpu.make_async_copy(mask_in, mask_ref, load_s.at[3]),
             pltpu.make_async_copy(right_in.at[0], raw.at[0], load_s.at[0]), pltpu.make_async_copy(left_in.at[0], raw.at[1], load_s.at[1])]
    for cp in loads:
        cp.start()

    hand = across == (r + 14) % 8
    active = core == x % 2
    even = z % 2 == yl
    home = yh == x // 2
    source = active & even & home
    odd = active & no(even) & home
    far = active & no(home)
    aside = (r % 8) // 4 != yl
    barrier = pltpu.get_barrier_semaphore()
    partners = [(r, (c + k) % 8) for k in range(1, 8)] + [(up, c), (down, c), (mirror, c), (twin, c)]
    for p in partners:
        pl.semaphore_signal(barrier, inc=1, device_id=p, device_id_type=MESH)

    @pl.when(far & even)
    def _():
        for j in range(4):
            pl.semaphore_signal(barrier, inc=1, device_id=(mirror, (1 - yl) * 4 + j), device_id_type=MESH)

    @pl.when((gap == 2) | hand)
    def _():
        for j in range(4):
            pl.semaphore_signal(barrier, inc=1, device_id=(mirror, (1 - yl) * 4 + j), device_id_type=MESH)
    for cp in loads:
        cp.wait()
    lane = lax.broadcasted_iota(jnp.int32, (128, 256), 1)
    for li in range(4):
        kept = lane < rank_ref[0, li]
        zero = jnp.zeros((128, 256), jnp.bfloat16)
        OWN[0, li] = jnp.where(kept, raw[0, li], zero)
        OWN[1, li] = jnp.where(kept, raw[1, li], zero)
    keep = [pltpu.make_async_copy(OWN.at[0], R.at[c], keep_s.at[0]), pltpu.make_async_copy(OWN.at[1], L.at[c], keep_s.at[1])]
    for cp in keep:
        cp.start()

    pl.semaphore_wait(barrier, len(partners) + 1 + jnp.where(aside, 1, 0))

    def send(src, dst, ss, rs, to):
        return pltpu.make_async_remote_copy(src_ref=src, dst_ref=dst, send_sem=ss, recv_sem=rs, device_id=to, device_id_type=MESH)

    order = [c, across, behind, ahead, (1 - yl) * 4 + (x + 3) % 4, (1 - yl) * 4 + (x + 1) % 4, yl * 4 + (x + 2) % 4, (1 - yl) * 4 + (x + 2) % 4]
    lo, hi = pl.ds(0, 2), pl.ds(2, 2)

    def row_copy(k, blk, part, to):
        v = R.at[blk] if part is None else R.at[blk, part]
        return send(OWN.at[0] if blk is order[0] else v, v, row_s, row_r.at[k], (r, to))

    row = [
        row_copy(0, order[0], None, across), row_copy(1, order[0], None, ahead), row_copy(2, order[0], None, behind),
        row_copy(3, order[1], None, ahead), row_copy(4, order[1], None, behind),
        row_copy(5, order[2], lo, ahead), row_copy(6, order[3], hi, behind),
        row_copy(7, order[4], lo, ahead), row_copy(8, order[5], hi, behind)]
    got = [
        row_copy(0, order[1], None, across), row_copy(1, order[2], None, ahead), row_copy(2, order[3], None, behind),
        row_copy(3, order[4], None, ahead), row_copy(4, order[5], None, behind),
        row_copy(5, order[6], lo, ahead), row_copy(6, order[6], hi, behind),
        row_copy(7, order[7], lo, ahead), row_copy(8, order[7], hi, behind)]

    mine, other = z // 2, 1 - z // 2
    below, above = ((z + 3) % 4) // 2, ((z + 1) % 4) // 2
    E, UP, DN = opts.get("parts", ((1, 4, 5, 7), (0, 3), (2, 6)))
    UW = UP + DN

    def move(src, dst, way, n, to): return send(src, dst, col_s.at[way], col_r.at[way, n], to)
    def r_block(k): return OWN.at[0] if k == 0 else R.at[order[k]]
    def r_copy(k, way): return send(r_block(k), C.at[mine, order[k]], col_s.at[way], col_r.at[way, k], ((up, down)[way], c))
    def c_copy(k, s, way, part=None):
        v = C.at[s, order[k]] if part is None else C.at[s, order[k], part]
        return move(v, v, way, k, ((up, down)[way], c))
    def cross(src, s, blk, n): return send(src, C.at[s, blk], col_s.at[2], mir_r.at[n], (mirror, c))
    def hold(_k):
        @pl.when(aside)
        def _():
            held.start()
    held = send(OWN.at[0], C.at[mine, c], hold_s, mir_r.at[x], (mirror, r % 8))
    def to_twin(src, s, blk): return send(src, C.at[s, blk], core_s, core_r, (twin, c))
    def own(k): return pltpu.make_async_copy(r_block(k), C.at[mine, order[k]], own_s.at[k])

    def col_source(k):
        @pl.when(source)
        def _():
            if k > 5:
                row_last(k)
            r_copy(k, 0).start(); r_copy(k, 1).start()
            own(k).start()
            to_twin(r_block(k), mine, order[k]).start()

    def row_step(k):
        if k == 1:
            got[0].wait_recv(); row[3].start(); row[4].start()
        elif k == 2:
            got[1].wait_recv(); row[5].start()
        elif k == 3:
            got[2].wait_recv(); row[6].start()
        elif k == 4:
            got[3].wait_recv(); row[7].start()
        elif k == 5:
            got[4].wait_recv(); row[8].start()
    def row_last(k):
        n = 2 * k - 7
        got[n].wait_recv(); got[n + 1].wait_recv()

    def row_rest(_k):
        for k in (6, 7):
            if do_col:
                @pl.when(no(source))
                def _():
                    row_last(k)
            else:
                row_last(k)

    def col_odd(k):
        @pl.when(odd)
        def _():
            for s, way, part, marks in ((below, 0, lo, UP), (above, 1, hi, DN)):
                c_copy(k, s, way).wait_recv()
                if k in marks:
                    cross(C.at[s, order[k]], s, order[k], UW.index(k)).start()
                c_copy(k, s, way, part).start()
                to_twin(C.at[s, order[k]], s, order[k]).start()

    def col_last(k):
        @pl.when(source)
        def _():
            c_copy(k, other, 0, lo).wait_recv(); c_copy(k, other, 1, hi).wait_recv()
            to_twin(C.at[other, order[k]], other, order[k]).start()

    def pick(flag, a, b): return jnp.where(flag, a, b)
    def far_own(i): return pick(even, mine, below if i < 2 else above), pick(even, order[E[i]], order[UW[i]])
    def far_down(i): return pick(even, other if i < 2 else mine, below), pick(even, order[UW[i]], order[E[i]])
    def far_up(i): return pick(even, mine if i < 2 else other, above), pick(even, order[UW[i]], order[E[i]])
    def far_next(i): return pick(even, other, above if i < 2 else below), far_own(i)[1]
    def far_copy(at, way, n, part=None):
        v = C.at[at[0], at[1]] if part is None else C.at[at[0], at[1], part]
        return move(v, v, way, n, ((up, down)[way], c))

    def far_first(i):
        @pl.when(far)
        def _():
            s, blk = far_own(i)
            cross(C.at[s, blk], s, blk, pick(even, blk % 4, i)).wait_recv()
            far_copy((s, blk), 0, i).start(); far_copy((s, blk), 1, i).start()
            to_twin(C.at[s, blk], s, blk).start()

    def far_pass(i):
        @pl.when(far)
        def _():
            for at, way, part in ((far_down(i), 0, lo), (far_up(i), 1, hi)):
                far_copy(at, way, i).wait_recv()
                far_copy(at, way, 4 + i, part).start()
                to_twin(C.at[at[0], at[1]], *at).start()

    def far_last(i):
        @pl.when(far)
        def _():
            at = far_next(i)
            far_copy(at, 0, 4 + i, lo).wait_recv(); far_copy(at, 1, 4 + i, hi).wait_recv()
            to_twin(C.at[at[0], at[1]], *at).start()

    def some(n, ss, part=None): return send(C.at[0, pl.ds(0, n)], C.at[0, pl.ds(0, n)], ss, core_r, (twin, c))

    def col_end():
        @pl.when(source)
        def _():
            some(8, col_s.at[0]).wait_send(); some(8, col_s.at[1]).wait_send()
        @pl.when(odd)
        def _():
            some(4, col_s.at[0]).wait_send(); some(4, col_s.at[1]).wait_send()
        @pl.when(far)
        def _():
            some(6, col_s.at[0]).wait_send(); some(6, col_s.at[1]).wait_send()
        @pl.when(odd)
        def _():
            some(4, col_s.at[2]).wait_send()
        @pl.when(aside)
        def _():
            held.wait_send()
        @pl.when(active)
        def _():
            send(C, C, core_s, core_r, (twin, c)).wait_send()

    ny = opts.get("ny", NY)
    first, rest = pl.ds(0, ny), pl.ds(ny, 4 - ny)
    targets = [(r + 8 - t) % 8 for t in range(3)]
    near_any = (targets[0] // 4 == yl) | (targets[1] // 4 == yl) | (targets[2] // 4 == yl)
    far_any = (targets[0] // 4 != yl) | (targets[1] // 4 != yl) | (targets[2] // 4 != yl)
    def left_near(t): return send(OWN.at[1], L.at[c], left_s.at[t], left_r.at[c], (r, targets[t]))
    def left_far(t): return send(OWN.at[1, rest], L.at[c, rest], left_s.at[t], left_r.at[c], (r, targets[t]))
    def left_over(): return send(OWN.at[1, first], L.at[c, first], over_s, over_r, (r, across))
    def left_on(t): return send(L.at[across, first], L.at[across, first], on_s.at[t], on_r.at[across], (r, targets[t]))
    def left_start(n):
        if n == 0 and ny:
            @pl.when(far_any)
            def _():
                left_over().start()
        for t, to in enumerate(targets):
            if n == 1:
                @pl.when((to != c) & (to // 4 == yl))
                def _():
                    left_near(t).start()
            if n == 2:
                @pl.when(to // 4 != yl)
                def _():
                    left_far(t).start()
    def left_turn(_k):
        if ny:
            @pl.when(near_any)
            def _():
                send(L.at[across, first], L.at[across, first], over_s, over_r, (r, across)).wait_recv()
            for t, to in enumerate(targets):
                @pl.when((to != c) & (to // 4 == yl))
                def _():
                    left_on(t).start()
    def left_end():
        if ny:
            @pl.when(far_any)
            def _():
                left_over().wait_send()
        for t, to in enumerate(targets):
            @pl.when((to != c) & (to // 4 == yl))
            def _():
                left_near(t).wait_send()
                if ny:
                    left_on(t).wait_send()
            @pl.when(to // 4 != yl)
            def _():
                left_far(t).wait_send()
    def left_got(k):
        blk = order[k]
        if k in (0,):
            return
        if k in (2, 3, 6):
            send(L.at[blk], L.at[blk], over_s, left_r.at[blk], (r, across)).wait_recv()
        else:
            send(L.at[blk, rest], L.at[blk, rest], over_s, left_r.at[blk], (r, across)).wait_recv()
            if ny and k != 1:
                send(L.at[blk, first], L.at[blk, first], over_s, on_r.at[blk], (r, across)).wait_recv()
    def l_twin(k): return send(OWN.at[1] if k == 0 else L.at[order[k]], J.at[order[k]], twin_s, twin_r, (twin, c))
    def j_twin(k): return send(J.at[order[k]], J.at[order[k]], twin_s, twin_r, (twin, c))
    def left_step(k):
        @pl.when(gap <= 2)
        def _():
            left_got(k)
        @pl.when((gap == 0) & (core == 0))
        def _():
            l_twin(k).start()

    goal = jnp.where(yh == 0, r, r + 12) % 8
    same = goal // 4 == yl
    lift = send(OWN.at[1], ZB, lift_s, lift_r, (up, c))
    def lift_start(_k):
        @pl.when(yh == 1)
        def _():
            lift.start()
    def part_from(src):
        return (send(src, XJ.at[x], next_s, relay_r.at[x], (mirror, (1 - goal // 4) * 4 + goal % 4)),
                send(src, J.at[c], next_s, next_r.at[c], (mirror, goal)))
    def part_start(k):
        @pl.when(yh == k)
        def _():
            if k == 1:
                lift.wait_recv()
            by, direct = part_from(ZB if k == 1 else OWN.at[1])
            @pl.when(same)
            def _():
                by.start()
            @pl.when(no(same))
            def _():
                direct.start()
    def relay(j): return send(XJ.at[j], J.at[(1 - yl) * 4 + j], relay_s, next_r.at[(1 - yl) * 4 + j], (r, across))
    def relay_step(j):
        @pl.when(hand)
        def _():
            send(XJ.at[j], XJ.at[j], relay_s, relay_r.at[j], (r, across)).wait_recv()
            relay(j).start()
    def next_step(k):
        @pl.when(gap == 2)
        def _():
            send(J.at[order[k]], J.at[order[k]], relay_s, next_r.at[order[k]], (r, across)).wait_recv()
        @pl.when((gap == 2) & (core == 1))
        def _():
            j_twin(k).start()
    def next_end():
        part_from(OWN.at[1])[1].wait_send()
        @pl.when(yh == 1)
        def _():
            lift.wait_send()
        @pl.when(hand)
        def _():
            send(XJ, XJ, relay_s, lift_r, (r, across)).wait_send()
        @pl.when(((gap == 0) & (core == 0)) | ((gap == 2) & (core == 1)))
        def _():
            send(J, J, twin_s, twin_r, (twin, c)).wait_send()
        @pl.when(gap == 1)
        def _():
            send(J, J, twin_s, twin_r, (twin, c)).wait_recv()

    shift = (r - gap - c) // 8
    has_tiles = gap <= 2
    def core_flip(_k):
        keep[0].wait()

        @pl.when(has_tiles)
        def _():
            for li in range(4):
                flipped[li] = R[:, li].reshape(1024, 256).T
    def core_copy(lj): return pltpu.make_async_copy(U.at[:, lj], U_out.at[0, 0, :, lj], out_s)
    def core_step(q, s):
        lj = 2 * q + s

        @pl.when(has_tiles)
        def _():
            right_j = C[s, :, q].reshape(1024, 256)
            wide = jnp.dot(flipped[q:].reshape((4 - q) * 256, 1024), right_j, preferred_element_type=jnp.float32)
            wide = wide.astype(jnp.bfloat16).reshape(4 - q, 256, 256)
            for li in range(q):
                U[li, lj] = jnp.zeros((256, 256), jnp.bfloat16)
            for li in range(q, 4):
                kept = (li * 16 + r >= lj * 8 + c) & (mask_ref[0, 0, li, lj] == 0)
                U[li, lj] = jnp.where(kept, wide[li - q], jnp.zeros((256, 256), jnp.bfloat16))

            @pl.when(shift == s)
            def _():
                M[q] = wide[0]
            if q < 3:
                @pl.when((shift == -1) & (s == 1))
                def _():
                    M[q + 1] = wide[1]
            core_copy(lj).start()
    def core_end():

        @pl.when(has_tiles)
        def _():
            picks = pltpu.make_async_copy(M, M_out, load_s.at[0])
            picks.start()
            pltpu.make_async_copy(U, U_out.at[0, 0], out_s).wait()
            picks.wait()
    def twin_wait(_k):
        @pl.when(source)
        def _():
            for k in range(8):
                own(k).wait()
        @pl.when(no(active))
        def _():
            send(C, C, core_s, core_r, (twin, c)).wait_recv()

    do_col, do_left = opts.get("col", True), opts.get("left", True)
    for cp in row[:3]:
        cp.start()
    steps = dict(r=row_step, q=row_rest)
    if do_col:
        steps.update(s=col_source, M=hold, o=col_odd, e=col_last, c=far_first, d=far_pass, h=far_last, t=twin_wait)
        steps.update(F=core_flip, A=lambda q: core_step(q, mine), B=lambda q: core_step(q, other))
    if do_left:
        steps.update(S=left_start, T=left_turn, l=left_step, n=next_step, Z=lift_start, J=part_start, x=relay_step)
    words = opts.get("order", ORDER)
    for word in (words.split() if isinstance(words, str) else words):
        if word[0] in steps:
            steps[word[0]](int(word[1:]))
    send(R.at[pl.ds(0, 7)], R.at[pl.ds(0, 7)], row_s, lift_r, (twin, c)).wait_send()
    keep[1].wait()
    if do_col:
        core_end()
    if do_left:
        left_end()
        next_end()
    if do_col:
        col_end()


bf = jnp.bfloat16
def D(*s): return pltpu.SemaphoreType.DMA(s)
B = (4, 128, 256)
SCRATCH = [pltpu.VMEM((4, 8, 256, 256), bf), pltpu.VMEM((4, 256, 256), bf),
           pltpu.VMEM((4, 256, 1024), bf), pltpu.VMEM((4,) + B, bf), pltpu.VMEM(B, bf), pltpu.VMEM((2,) + B, bf),
           pltpu.VMEM((2,) + B, bf), pltpu.SMEM((1, 4), jnp.int32), pltpu.SMEM((1, 1, 4, 8), jnp.int32), D(4), D(),
           D(), D(9), D(3), D(2, 8), D(4), D(), D(),
           D(3), D(8), D(), D(8), D(), D(4), D(), D(), D(), D(), D(8), D(2), D(), D(), D(3), D(8), D()]
OUTS = [(1, 1, 4, 8, 256, 256), (4, 256, 256), (8,) + B, (8,) + B, (8,) + B, (2, 8) + B]


def gather(panel_left, panel_right, panel_ranks, dense_mask, opts={}, vm=12):
    return pl.pallas_call(
        functools.partial(gather_kernel, opts=opts),
        out_shape=tuple(jax.ShapeDtypeStruct(s, bf) for s in OUTS[:4]) + tuple(pltpu.VMEM(s, bf) for s in OUTS[4:]),
        in_specs=[pl.BlockSpec(memory_space=pltpu.HBM)] * 4,
        out_specs=(pl.BlockSpec(memory_space=pl.ANY),) * 4 + (pl.BlockSpec(memory_space=pltpu.VMEM),) * 2,
        scratch_shapes=SCRATCH,
        compiler_params=pltpu.CompilerParams(collective_id=0, has_side_effects=True, vmem_limit_bytes=vm << 20),
        cost_estimate=pl.CostEstimate(flops=20_000_000_000, bytes_accessed=100_000_000, transcendentals=0),
        name="gather_cores",
    )(*(pltpu.with_memory_space_constraint(v, pltpu.HBM) for v in (panel_left, panel_right, panel_ranks, dense_mask)))


def update_kernel(U, M, L, J, R, C, mask_ref, tiles, core_out, dense_out,
                  dense, panels, lean, flipped, masked, core_sem, dense_sem):
    r, c = lax.axis_index("row"), lax.axis_index("col")
    gap = (r + 8 - c) % 8
    has_tiles = gap <= 2
    shift = (r - gap - c) // 8

    def dense_back(li): return pltpu.make_async_copy(dense.at[li], dense_out.at[0, 0, li], dense_sem.at[li])
    def zero_back(li): return pltpu.make_async_copy(dense.at[0], dense_out.at[0, 0, li], dense_sem.at[li])
    core_back = pltpu.make_async_copy(U, core_out, core_sem)

    @pl.when(jnp.logical_not(has_tiles))
    def _():
        dense[0] = jnp.zeros((1024, 1024), jnp.bfloat16)
        for li in range(4):
            zero_back(li).start()
        for li in range(4):
            flipped[li] = R[:, li].reshape(1024, 256).T
        for lj in range(8):
            first = lj // 2
            right_j = C[lj % 2, :, first].reshape(1024, 256)
            wide = jnp.dot(flipped[first:].reshape((4 - first) * 256, 1024), right_j, preferred_element_type=jnp.float32)
            wide = wide.astype(jnp.bfloat16).reshape(4 - first, 256, 256)
            for li in range(4):
                if li < first:
                    masked[li, lj] = jnp.zeros((256, 256), jnp.bfloat16)
                else:
                    kept = (li * 16 + r >= lj * 8 + c) & (mask_ref[0, 0, li, lj] == 0)
                    masked[li, lj] = jnp.where(kept, wide[li - first], jnp.zeros((256, 256), jnp.bfloat16))
            pltpu.make_async_copy(masked.at[:, lj], core_out.at[0, 0, :, lj], core_sem).start()

    @pl.when(has_tiles)
    def _():
        core_back.start()
        for li in range(4):
            lj = 2 * li + shift
            there = (lj >= 0) & (mask_ref[0, 0, li, jnp.maximum(lj, 0)] > 0)
            lj_row = jnp.maximum(li - jnp.where(r < gap, 1, 0), 0)
            lean[...] = jnp.dot(L[:, li].reshape(1024, 256), M[li], preferred_element_type=jnp.float32).astype(jnp.bfloat16)

            @pl.when(gap == 0)
            def _():
                panels[...] = L[:, li].reshape(1024, 256)

            @pl.when(gap > 0)
            def _():
                panels[...] = J[:, lj_row].reshape(1024, 256)
            for part in range(4):
                rows = pl.ds(part * 256, 256)
                change = lax.dot_general(lean[rows], panels[...], (((1,), (1,)), ((), ())), preferred_element_type=jnp.float32)
                new = (tiles[0, 0, li, rows].astype(jnp.float32) - change).astype(jnp.bfloat16)
                dense[li, rows] = jnp.where(there, new, jnp.zeros_like(new))
                pltpu.make_async_copy(dense.at[li, rows], dense_out.at[0, 0, li, rows], dense_sem.at[li]).start()

    core_back.wait()
    for li in range(4):
        dense_back(li).wait()


def update(U, M, L, J, R, C, dense_mask, dense_tiles):
    V, A = pl.BlockSpec(memory_space=pltpu.VMEM), pl.BlockSpec(memory_space=pl.ANY)
    return pl.pallas_call(
        update_kernel,
        out_shape=(jax.ShapeDtypeStruct((1, 1, 4, 8, 256, 256), bf), jax.ShapeDtypeStruct((1, 1, 4, 1024, 1024), bf)),
        in_specs=[A, V, V, V, V, V, pl.BlockSpec(memory_space=pltpu.SMEM), V],
        out_specs=(A, A),
        scratch_shapes=[pltpu.VMEM((4, 1024, 1024), bf), pltpu.VMEM((1024, 256), bf), pltpu.VMEM((1024, 256), bf),
                        pltpu.VMEM((4, 256, 1024), bf), pltpu.VMEM((4, 8, 256, 256), bf), D(), D(4)],
        compiler_params=pltpu.CompilerParams(vmem_limit_bytes=20 << 20),
        cost_estimate=pl.CostEstimate(flops=3_000_000_000, bytes_accessed=20_000_000, transcendentals=0),
        name="update_tiles",
    )(U, M, L, J, *(pltpu.with_memory_space_constraint(v, pltpu.VMEM) for v in (R, C)), dense_mask, dense_tiles)


def per_device(panel_left, panel_right, panel_ranks, dense_mask, dense_tiles):
    U, M, L, J, R, C = gather(panel_left, panel_right, panel_ranks, dense_mask)
    return update(U, M, L, J, R, C, dense_mask, dense_tiles)


def solution(mesh):
    placed = (
        P("row", None, "col", None),
        P("row", None, "col", None),
        P("row", None),
        P("row", "col", None, None),
        P("row", "col", None, None, None),
    )
    return jax.shard_map(
        per_device,
        mesh=mesh,
        in_specs=placed,
        out_specs=(P("row", "col", None, None, None, None), P("row", "col", None, None, None)),
        check_vma=False,
    )
```
